512 devices in a mesh: block: 32 (over z_lo, y, core), row: 16 (over x, z_hi).
Axes of the slice: x: 4, y: 4, z: 16 (z_hi: 4, z_lo: 4; z = z_hi * 4 + z_lo), core: 2. Of those that a mesh axis runs over, the one named last changes fastest.
Arguments:
- embed: float32 [196608, 128], P(('block', 'row'))
- partner: int32 [196608], P(('block', 'row')), may hold values from 0 to 6143, as said below
- plan: int32 [2, 32], replicated, may hold values from 0 to 31, as said below
Outputs:
- grad: float32 [196608, 128], P(('block', 'row'))
- log_partition: float32 [196608], P(('block', 'row'))
- loss: float32 [], replicated
The draws below stay inside these ranges and needn't reach their ends.
Inputs may be any that keep to these rules, and one draw needn't show every extreme that they name: The pairing is mutual within each block: the partner of the partner of a view is the view itself, and no view is its own partner. `plan`: each row pairs all 32 blocks: entry b names the opponent of block b, the opponent's entry names b, no entry names its own block, and no two blocks meet in two rows.
All inputs are finite; a program needn't handle non-finite values.
Results may differ from the reference program's by a relative error of at most 0.0025.
The reference program's roundings to bfloat16 on the way count: a program that leaves them out, or rounds other values in their place, can miss the bound.
Values may be sent and summed in bfloat16 or wider, within the bound.
No kernel may reach another device: no remote copies, remote signals or barrier semaphores. Data moves between devices by JAX's collectives and lax.ppermute only.
A program may use at most 128 MiB of HBM per device.

```python
import jax
import jax.numpy as jnp
from jax import lax

E = 128
R_DEV = 384
ROUNDS = 2
BLOCK_ROWS = 6144
VIEWS = 196608
N_BLOCK = 32


def pair_table(key):
    perms = jax.vmap(lambda sub: jax.random.permutation(sub, BLOCK_ROWS))(jax.random.split(key, N_BLOCK))
    perms = perms.astype(jnp.int32)
    other = perms.reshape(N_BLOCK, BLOCK_ROWS // 2, 2)[:, :, ::-1].reshape(N_BLOCK, BLOCK_ROWS)
    table = jnp.zeros((N_BLOCK, BLOCK_ROWS), jnp.int32)
    table = table.at[jnp.arange(N_BLOCK, dtype=jnp.int32)[:, None], perms].set(other)
    return table


def draw_partner(key, part):
    table = pair_table(key)
    return table.reshape(VIEWS).astype(jnp.int32)


def draw_plan(key, part):
    key = jax.random.fold_in(key, 5)
    first, second = jax.random.split(key)
    chosen = jax.random.permutation(first, N_BLOCK - 1)[:ROUNDS].astype(jnp.int32)
    sigma = jax.random.permutation(second, N_BLOCK).astype(jnp.int32)
    places = jnp.arange(N_BLOCK, dtype=jnp.int32)

    def one_round(turn):
        mirror = (2 * turn - places) % (N_BLOCK - 1)
        opposite = jnp.where(places == N_BLOCK - 1, turn, jnp.where(places == turn, N_BLOCK - 1, mirror))
        return jnp.zeros((N_BLOCK,), jnp.int32).at[sigma].set(sigma[opposite])
    return jax.vmap(one_round)(chosen).astype(jnp.int32)


def draw_embed(key, part):
    table = pair_table(key)
    key = jax.random.fold_in(key, 7)
    first = jax.random.fold_in(key, 0)
    second = jax.random.fold_in(key, 1)
    third = jax.random.fold_in(key, 2)
    fifth = jax.random.fold_in(key, 4)
    sixth = jax.random.fold_in(key, 5)
    seventh = jax.random.fold_in(key, 6)
    centres = jax.random.normal(third, (8, E), jnp.float32)
    cluster_top = jax.random.uniform(fifth, (8,), jnp.float32, 0.3, 2.4)
    cluster_index = jax.random.randint(sixth, (VIEWS,), 0, 8).astype(jnp.int32)
    chosen_centre = centres[cluster_index]
    cluster_strength = cluster_top[cluster_index][:, None]
    group_weight = jax.random.uniform(seventh, (VIEWS // R_DEV, 1), jnp.float32, 0.1, 1.0)
    mate_weight = jnp.repeat(group_weight, R_DEV, axis=0)
    noise = jax.random.normal(first, (VIEWS, E), jnp.float32)
    strength = jax.random.uniform(second, (VIEWS, 1), jnp.float32, 0.0, 1.0) * cluster_strength
    mate = (table + jnp.arange(N_BLOCK, dtype=jnp.int32)[:, None] * BLOCK_ROWS).reshape(VIEWS)
    paired = noise[mate]
    return (0.9 * noise + mate_weight * paired + strength * chosen_centre).astype(jnp.float32)


def setup_inputs(seed: int = 0) -> dict:
    key_list = jax.random.split(jax.random.key(seed), 4)
    return {
        "embed": draw_embed(jax.random.fold_in(key_list[3], 71), 0),
        "partner": draw_partner(jax.random.fold_in(key_list[3], 71), 0),
        "plan": draw_plan(jax.random.fold_in(key_list[3], 71), 0),
    }


inverse_tau = 10.0

def reference(embed, partner, plan):
    inverse = lax.rsqrt(lax.optimization_barrier(jnp.sum(embed * embed, axis=1, keepdims=True)) + 1e-06)
    unit = embed * inverse
    rounded_values = unit.astype(jnp.bfloat16)
    blocks = rounded_values.reshape(N_BLOCK, BLOCK_ROWS, E)
    mates = partner.reshape(N_BLOCK, BLOCK_ROWS)
    position = jnp.arange(BLOCK_ROWS, dtype=jnp.int32)
    self_mask = position[:, None] == position[None, :]

    def key_blocks(index):
        return jnp.concatenate([index[None], plan[:, index]]).astype(jnp.int32)

    def lse_block(index):
        anchor_embeddings = blocks[index]
        ids = key_blocks(index)
        contrastive_objective = jnp.zeros((BLOCK_ROWS,), jnp.float32)
        for turn in range(ROUNDS + 1):
            candidate_embeddings = blocks[ids[turn]]
            similarity_grid = jnp.dot(anchor_embeddings, candidate_embeddings.T, preferred_element_type=jnp.float32) * inverse_tau
            similarity_exps = jnp.exp(similarity_grid - inverse_tau)
            if turn == 0:
                similarity_exps = jnp.where(self_mask, 0.0, similarity_exps)
            contrastive_objective = contrastive_objective + lax.optimization_barrier(jnp.sum(similarity_exps, axis=1))
        return inverse_tau + jnp.log(contrastive_objective)
    log_partition = lax.map(lse_block, jnp.arange(N_BLOCK, dtype=jnp.int32))

    def positive_block(index):
        anchor_embeddings = blocks[index].astype(jnp.float32)
        partner_embedding_block = blocks[index][mates[index]].astype(jnp.float32)
        return inverse_tau * lax.optimization_barrier(jnp.sum(anchor_embeddings * partner_embedding_block, axis=1))
    matched_similarity = lax.map(positive_block, jnp.arange(N_BLOCK, dtype=jnp.int32))
    loss = jnp.mean(log_partition - matched_similarity)

    def grad_block(index):
        anchor_embeddings = blocks[index]
        ids = key_blocks(index)
        query_lse = log_partition[index]
        contrastive_objective = jnp.zeros((BLOCK_ROWS, E), jnp.float32)
        for turn in range(ROUNDS + 1):
            candidate_embeddings = blocks[ids[turn]]
            key_lse = log_partition[ids[turn]]
            similarity_grid = jnp.dot(anchor_embeddings, candidate_embeddings.T, preferred_element_type=jnp.float32) * inverse_tau
            weight = jnp.exp(similarity_grid - query_lse[:, None]) + jnp.exp(similarity_grid - key_lse[None, :])
            if turn == 0:
                weight = jnp.where(self_mask, 0.0, weight)
            contrastive_objective = contrastive_objective + jnp.dot(weight.astype(jnp.bfloat16), candidate_embeddings, preferred_element_type=jnp.float32)
        partner_embedding_block = blocks[index][mates[index]].astype(jnp.float32)
        return inverse_tau * (contrastive_objective - 2.0 * partner_embedding_block)
    normalized_embedding = lax.map(grad_block, jnp.arange(N_BLOCK, dtype=jnp.int32)).reshape(VIEWS, E)
    grad = inverse * (normalized_embedding - unit * lax.optimization_barrier(jnp.sum(unit * normalized_embedding, axis=1, keepdims=True)))
    return (grad, log_partition.reshape(VIEWS), loss)
```

```python
import functools

import jax
import jax.numpy as jnp
import numpy as np
from jax import lax
from jax.experimental import pallas as pl
from jax.experimental.pallas import tpu as pltpu
from jax.sharding import Mesh
from jax.sharding import PartitionSpec as P

ROUNDS = 2
INVERSE_TAU = 10.0
LOG2E = float(np.log2(np.e))
SCALE = INVERSE_TAU * LOG2E

AXES = ("zl", "y", "c", "x", "zh")
SIZES = (4, 4, 2, 4, 4)
BLOCK = ("zl", "y", "c")
COLUMN = ("zh", "zl")
PLANE = ("y", "c", "x")

R = 384
E = 128
N_BLOCK = 32
N_X = 4
N_ZH = 4
N_ZL = 4
BLOCK_ROWS = R * N_X * N_ZH
CHUNK = 16
KEYS = 3 * R
PACK = KEYS + 16
OUT = R + 16
VMEM = 56 * 1024 * 1024

whole = pl.BlockSpec(memory_space=pltpu.VMEM)
smem = pl.BlockSpec(memory_space=pltpu.SMEM)


def to_column(row):
    return jnp.transpose(jnp.broadcast_to(row, (E, R)))


def lanes(wide):
    return jnp.concatenate([wide] * (R // E), axis=1)


def partner_row(keys_ref, xp):
    parts = keys_ref[xp, KEYS:PACK, :].astype(jnp.float32)
    pieces = [parts[i : i + 1] * 128.0 + parts[3 + i : 4 + i] for i in range(3)]
    return jnp.concatenate(pieces, axis=1).astype(jnp.int32)


def select_kernel(plan_ref, chunks_ref, out_ref):
    for b in range(N_BLOCK):
        for t in range(ROUNDS):
            out_ref[b, t] = chunks_ref[plan_ref[t, b]]


def pack_kernel(rounded_ref, opponents_ref, partner_ref, out_ref):
    index = partner_ref[...]
    high = index // 128
    low = index - high * 128
    both = jnp.concatenate([high, low, jnp.zeros((10, E), jnp.int32)], axis=0)
    index = both.astype(jnp.float32).astype(jnp.bfloat16)
    for xp in range(N_X):
        out_ref[xp, 0:R] = rounded_ref[...]
        for t in range(ROUNDS):
            for k in range(R // CHUNK):
                at = (t + 1) * R + k * CHUNK
                out_ref[xp, at : at + CHUNK] = opponents_ref[k, t]
        out_ref[xp, KEYS:PACK] = index


def partition_kernel(queries_ref, keys_ref, exp_ref, sums_ref, positive_ref):
    piece = pl.program_id(0)
    x = lax.axis_index("x")
    zh = lax.axis_index("zh")
    q = queries_ref[(zh - piece + N_ZH) % N_ZH]
    base = x * (R * N_ZH) + piece * R
    row = lax.broadcasted_iota(jnp.int32, (R, R), 0)
    diagonal = row - lax.broadcasted_iota(jnp.int32, (R, R), 1)
    total = jnp.zeros((R, E), jnp.float32)
    positive = jnp.zeros((R, E), jnp.float32)
    for xp in range(N_X):
        for t in range(ROUNDS + 1):
            k = keys_ref[xp, t * R : (t + 1) * R, :]
            s = lax.dot_general(q, k, (((1,), (1,)), ((), ())), preferred_element_type=jnp.float32)
            e = jnp.exp2(s * SCALE - SCALE)
            if t == 0:
                e = jnp.where(diagonal == xp * (R * N_ZH) + zh * R - base, 0.0, e)
                mine = jnp.where(row == partner_row(keys_ref, xp) - base, s, 0.0)
                for i in range(R // E):
                    positive = positive + mine[:, i * E : (i + 1) * E]
            for i in range(R // E):
                total = total + e[:, i * E : (i + 1) * E]
            at = (xp * 3 + t) * R
            exp_ref[:, at : at + R] = e.astype(jnp.bfloat16)
    sums_ref[0] = lax.dot_general(
        jnp.ones((8, E), jnp.float32), total, (((1,), (1,)), ((), ())),
        precision=lax.Precision.HIGHEST, preferred_element_type=jnp.float32,
    )

    @pl.when(piece == 0)
    def _():
        positive_ref[...] = jnp.zeros_like(positive_ref)

    positive_ref[...] += jnp.sum(positive.reshape(R // 8, 8, E), axis=0)


def direction_kernel(plan_ref, exp_ref, queries_ref, keys_ref, own_ref, sums_ref, out_ref):
    piece = pl.program_id(0)
    zl, y, c = (lax.axis_index(a) for a in BLOCK)
    x = lax.axis_index("x")
    zh = lax.axis_index("zh")
    here = (zl * 4 + y) * 2 + c
    q = queries_ref[(zh - piece + N_ZH) % N_ZH]
    base = x * (R * N_ZH) + piece * R
    row = lax.broadcasted_iota(jnp.int32, (R, R), 0)
    column = lanes(to_column(1.0 / own_ref[pl.ds(piece, 1), :]))
    total = jnp.zeros((R, E), jnp.float32)
    for t in range(ROUNDS + 1):
        other = here if t == 0 else plan_ref[t - 1, here]
        level = other // 8
        place = other - level * 8
        for xp in range(N_X):
            k = keys_ref[xp, t * R : (t + 1) * R, :]
            at = (xp * 3 + t) * R
            inverse = 1.0 / sums_ref[pl.ds(place * N_X + xp, 1), pl.ds(pl.multiple_of(level * R, 128), R)]
            w = exp_ref[:, at : at + R].astype(jnp.float32) * (column + inverse)
            if t == 0:
                w = w - jnp.where(row == partner_row(keys_ref, xp) - base, 2.0, 0.0)
            total = total + jnp.dot(w.astype(jnp.bfloat16), k, preferred_element_type=jnp.float32)
    wide = q.astype(jnp.float32)
    along = jnp.sum(total * wide, axis=1, keepdims=True).astype(jnp.bfloat16).astype(jnp.float32)
    out_ref[0, 0:R] = (total - along * wide).astype(jnp.bfloat16)
    first = lax.broadcasted_iota(jnp.int32, (R, E), 1) == 0
    line = lax.dot_general(
        jnp.ones((8, E), jnp.bfloat16), jnp.where(first, along, 0.0).astype(jnp.bfloat16),
        (((1,), (1,)), ((), ())), preferred_element_type=jnp.float32,
    )
    line = [line[0:1, i * E : (i + 1) * E] for i in range(R // E)]
    line = jnp.concatenate(line + [jnp.zeros((16 - R // E, E), jnp.float32)], axis=0)
    out_ref[0, R:OUT] = line.astype(jnp.bfloat16)


def finish_kernel(embed_ref, parts_ref, out_ref):
    x = embed_ref[...]
    inverse = lax.rsqrt(jnp.sum(x * x, axis=1, keepdims=True) + 1e-06)
    unit = x * inverse
    rounded = unit.astype(jnp.bfloat16).astype(jnp.float32)
    total = jnp.zeros((R, E), jnp.float32)
    line = jnp.zeros((16, E), jnp.float32)
    for z in range(N_ZH):
        total = total + parts_ref[z, 0:R].astype(jnp.float32)
        line = line + parts_ref[z, R:OUT].astype(jnp.float32)
    along = to_column(jnp.concatenate([line[i : i + 1] for i in range(R // E)], axis=1))
    direction = INVERSE_TAU * (total + along * rounded)
    out_ref[...] = inverse * (direction - unit * jnp.sum(unit * direction, axis=1, keepdims=True))


def params(**more):
    return pltpu.CompilerParams(vmem_limit_bytes=VMEM, **more)


def f32(*shape):
    return jax.ShapeDtypeStruct(shape, jnp.float32)


def bf16(*shape):
    return jax.ShapeDtypeStruct(shape, jnp.bfloat16)


def exchange(value, axes):
    return lax.all_to_all(value, axes, 0, 0, tiled=True)


def body(embed, partner, plan):
    zl = lax.axis_index("zl")
    zh = lax.axis_index("zh")
    with jax.named_scope("normalize"):
        inverse = lax.rsqrt(jnp.sum(embed * embed, axis=1, keepdims=True) + 1e-06)
        rounded = (embed * inverse).astype(jnp.bfloat16)
    with jax.named_scope("queries"):
        queries = [rounded]
        for shift in (1, 2, 3):
            queries.append(lax.ppermute(rounded, "zh", [(i, (i + shift) % N_ZH) for i in range(N_ZH)]))
        queries = jnp.stack(queries)
    with jax.named_scope("opponents"):
        padded = jnp.concatenate([rounded, rounded[: N_BLOCK * CHUNK - R]])
        chunks = exchange(padded.reshape(N_BLOCK, CHUNK, E), BLOCK)
        chosen = pl.pallas_call(
            select_kernel, out_shape=bf16(N_BLOCK, ROUNDS, CHUNK, E), in_specs=[smem, whole], out_specs=whole,
            compiler_params=params(),
        )(plan, chunks)
        chosen = exchange(chosen, BLOCK)
    with jax.named_scope("keys"):
        packed = pl.pallas_call(
            pack_kernel, out_shape=bf16(N_X, PACK, E), in_specs=[whole] * 3, out_specs=whole,
            compiler_params=params(),
        )(rounded, chosen, partner.reshape(3, 128))
        keys = exchange(packed, "x")
    with jax.named_scope("partition"):
        exps, sums, positive = pl.pallas_call(
            partition_kernel,
            grid=(N_ZH,),
            out_shape=(bf16(N_ZH * R, N_X * KEYS), f32(N_ZH, 8, R), f32(8, E)),
            in_specs=[whole, whole],
            out_specs=(
                pl.BlockSpec((R, N_X * KEYS), lambda g: (g, 0)),
                pl.BlockSpec((1, 8, R), lambda g: (g, 0, 0)),
                pl.BlockSpec((8, E), lambda g: (0, 0)),
            ),
            compiler_params=params(),
        )(queries, keys)
    with jax.named_scope("sums"):
        line = jnp.concatenate([sums[:, 0, :].reshape(N_ZH * R), jnp.full((E,), jnp.sum(positive))])
        line = exchange(jnp.broadcast_to(line, (N_ZH * N_ZL, N_ZH * R + E)), COLUMN)
        line = jnp.sum(line.reshape(N_ZH, N_ZL, N_ZH * R + E), axis=0)
        parts = line[:, : N_ZH * R].reshape(N_ZL, N_ZH, R)
        mine = lax.dynamic_index_in_dim(parts, zl, 0, keepdims=False)
        log_partition = INVERSE_TAU + jnp.log(lax.dynamic_index_in_dim(mine, zh, 0, keepdims=False))
        column_loss = jnp.sum(INVERSE_TAU + jnp.log(parts)) - INVERSE_TAU * jnp.sum(line[:, N_ZH * R])
        level = lax.dynamic_index_in_dim(parts, zh, 1, keepdims=False).reshape(N_ZL * R)
        level = jnp.concatenate([level, jnp.full((E,), column_loss)])
        level = exchange(jnp.broadcast_to(level, (32, N_ZL * R + E)), PLANE)
        loss = jnp.sum(level[:, N_ZL * R]) / (N_BLOCK * BLOCK_ROWS)
    with jax.named_scope("direction"):
        out = pl.pallas_call(
            direction_kernel,
            grid=(N_ZH,),
            out_shape=bf16(N_ZH, OUT, E),
            in_specs=[smem, pl.BlockSpec((R, N_X * KEYS), lambda g: (g, 0)), whole, whole, whole, whole],
            out_specs=pl.BlockSpec((1, OUT, E), lambda g: (g, 0, 0)),
            compiler_params=params(),
        )(plan, exps, queries, keys, mine, level)
        out = exchange(out, "zh")
    with jax.named_scope("finish"):
        grad = pl.pallas_call(
            finish_kernel, out_shape=f32(R, E), in_specs=[whole] * 2, out_specs=whole, compiler_params=params(),
        )(embed, out)
    return (grad, log_partition, loss)


def solution(mesh):
    split = Mesh(mesh.devices.reshape(SIZES), AXES)
    return jax.shard_map(
        body,
        mesh=split,
        in_specs=(P(AXES, None), P(AXES), P()),
        out_specs=(P(AXES, None), P(AXES), P()),
        check_vma=False,
    )
```

```python
import jax
import jax.numpy as jnp
import numpy as np
from jax import lax
from jax.experimental import pallas as pl
from jax.experimental.pallas import tpu as pltpu
from jax.sharding import Mesh
from jax.sharding import PartitionSpec as P

ROUNDS = 2
INVERSE_TAU = 10.0
SCALE = INVERSE_TAU * float(np.log2(np.e))

AXES = ("zl", "y", "c", "x", "zh")
SIZES = (4, 4, 2, 4, 4)
BLOCK = ("zl", "y", "c")
PLANE = ("y", "x", "c")
COLUMN = ("zh", "zl")

R = 384
E = 128
N_BLOCK = 32
N_X = 4
N_ZL = 4
N_ZH = 4
GATHERED = R * N_ZH
BLOCK_ROWS = GATHERED * N_X
CHUNK = GATHERED // N_BLOCK
SENT = R + 16
LINES = R // E
SLOT = LINES * N_X
NEAR = 8
LOSS = LINES * NEAR
VMEM = 56 * 1024 * 1024

whole = pl.BlockSpec(memory_space=pltpu.VMEM)
smem = pl.BlockSpec(memory_space=pltpu.SMEM)


def as_row(lines):
    return jnp.concatenate([lines[i : i + 1] for i in range(LINES)], axis=1)


def as_lines(row):
    return jnp.concatenate([row[0:1, i * E : (i + 1) * E] for i in range(LINES)], axis=0)


def to_column(row):
    return jnp.transpose(jnp.broadcast_to(row, (E, R)))


def widen(wide):
    return jnp.concatenate([wide] * LINES, axis=1)


def lane_sums(value):
    return lax.dot_general(
        jnp.ones((8, E), jnp.float32), value, (((1,), (1,)), ((), ())),
        precision=lax.Precision.HIGHEST, preferred_element_type=jnp.float32,
    )


def scores(q, k):
    return lax.dot_general(q, k, (((1,), (1,)), ((), ())), preferred_element_type=jnp.float32)


def normalize_kernel(embed_ref, partner_ref, rounded_ref, sent_ref):
    x = embed_ref[...]
    inverse = lax.rsqrt(jnp.sum(x * x, axis=1, keepdims=True) + 1e-06)
    rounded = (x * inverse).astype(jnp.bfloat16)
    rounded_ref[...] = rounded
    index = partner_ref[...]
    high = index // 128
    low = index - high * 128
    both = jnp.concatenate([high, low, jnp.zeros((16 - 2 * LINES, E), jnp.int32)], axis=0)
    index = both.astype(jnp.float32).astype(jnp.bfloat16)
    for xp in range(N_X):
        sent_ref[xp, 0:R] = rounded
        sent_ref[xp, R:SENT] = index


def select_kernel(plan_ref, chunks_ref, queries_ref, out_ref):
    for b in range(N_BLOCK):
        for t in range(ROUNDS):
            out_ref[b, t] = chunks_ref[plan_ref[t, b]]


def own_kernel(queries_ref, keys_ref, exp_ref, match_ref, sums_ref):
    piece = pl.program_id(0)
    x = lax.axis_index("x")
    zh = lax.axis_index("zh")
    q = queries_ref[0, 0:R]
    index = queries_ref[0, R:SENT].astype(jnp.float32)
    index = as_row(index[0:LINES]) * 128.0 + as_row(index[LINES : 2 * LINES])
    partner = widen(to_column(index)).astype(jnp.int32) - x * GATHERED
    lane = lax.broadcasted_iota(jnp.int32, (R, R), 1)
    itself = lax.broadcasted_iota(jnp.int32, (R, R), 0) + (piece - x) * GATHERED + zh * R
    total = jnp.zeros((R, E), jnp.float32)
    match = jnp.zeros((R, E), jnp.float32)
    for z in range(N_ZH):
        k = keys_ref[z * R : (z + 1) * R]
        e = jnp.exp2(scores(q, k) * SCALE - SCALE)
        e = jnp.where(itself - lane == z * R, 0.0, e)
        for i in range(LINES):
            total = total + e[:, i * E : (i + 1) * E]
        exp_ref[:, z * R : (z + 1) * R] = e.astype(jnp.bfloat16)
        chosen = jnp.where(partner - lane == z * R, 1.0, 0.0).astype(jnp.bfloat16)
        match = match + jnp.dot(chosen, k, preferred_element_type=jnp.float32)
    match_ref[...] = match
    positive = jnp.sum((match * q.astype(jnp.float32)).reshape(R // 8, 8, E), axis=0)
    positive = jnp.broadcast_to(jnp.sum(positive, axis=(0, 1), keepdims=True), (8, R))
    slot = lax.broadcasted_iota(jnp.int32, (8, R), 0)
    sums_ref[0] = jnp.where(slot == 0, lane_sums(total), positive)


def others_kernel(queries_ref, keys_ref, own_ref, exp_ref, line_ref):
    piece = pl.program_id(0)
    q = queries_ref[0, 0:R]
    total = jnp.zeros((R, E), jnp.float32)
    for t in range(ROUNDS):
        for z in range(N_ZH):
            k = jnp.concatenate([keys_ref[z * 8 + i, t] for i in range(8)], axis=0)
            e = jnp.exp2(scores(q, k) * SCALE - SCALE)
            for i in range(LINES):
                total = total + e[:, i * E : (i + 1) * E]
            at = (t * N_ZH + z) * R
            exp_ref[:, at : at + R] = e.astype(jnp.bfloat16)

    @pl.when(piece == 0)
    def _():
        line_ref[...] = jnp.zeros_like(line_ref)

    sums = lane_sums(total)[0:1] + own_ref[0, 0:1]
    sums = as_lines(sums)
    slot = lax.broadcasted_iota(jnp.int32, (16, E), 0)
    line = jnp.where(slot == SLOT, jnp.broadcast_to(own_ref[0, 1:2, 0:E], (16, E)), 0.0)
    for i in range(LINES):
        line = jnp.where(slot == piece * LINES + i, jnp.broadcast_to(sums[i : i + 1], (16, E)), line)
    for i in range(N_BLOCK):
        line_ref[i] += line


def sums_kernel(line_ref, level_ref, mine_ref, log_ref, held):
    near = lax.axis_index("y") * 2 + lax.axis_index("c")
    x = lax.axis_index("x")
    slot = lax.broadcasted_iota(jnp.int32, (16, E), 0)
    loss = jnp.zeros((16, E), jnp.float32)
    for i in range(NEAR):
        y, c = divmod(i, 2)
        part = line_ref[y * 8 + c]
        for j in range(1, N_X):
            part = part + line_ref[y * 8 + j * 2 + c]
        sums = jnp.where(slot < SLOT, part, 1.0)
        logs = INVERSE_TAU + jnp.log(sums)
        loss = loss + jnp.where(slot < SLOT, logs, 0.0)
        loss = loss - jnp.where(slot == SLOT, part * (INVERSE_TAU / E), 0.0)
        held[i, 0] = 1.0 / sums
        held[i, 1] = logs
    mine_ref[...] = held[near, 0]
    log_ref[...] = held[near, 1, pl.ds(x * LINES, LINES), :]
    level = [held[i, 0, pl.ds(x * LINES, LINES), :] for i in range(NEAR)]
    loss = jnp.broadcast_to(jnp.sum(loss, axis=(0, 1), keepdims=True), (1, E))
    for _ in range(3):
        level.append(loss.astype(jnp.bfloat16).astype(jnp.float32))
        loss = loss - level[-1]
    level.append(jnp.zeros((32 - LOSS - 3, E), jnp.float32))
    level = jnp.concatenate(level, axis=0).astype(jnp.bfloat16)
    for i in range(N_ZH * N_ZL):
        level_ref[i] = level


def direction_kernel(plan_ref, own_ref, others_ref, keys_ref, far_ref, match_ref, mine_ref, sums_ref, out_ref, held, both):
    piece = pl.program_id(0)

    @pl.when(piece == 0)
    def _():
        zl, y, c = (lax.axis_index(a) for a in BLOCK)
        here = (zl * 4 + y) * 2 + c
        held[...] = sums_ref[...].astype(jnp.float32)
        for t in range(ROUNDS + 1):
            other = here if t == 0 else plan_ref[t - 1, here]
            level = other // NEAR
            near = other - level * NEAR
            for z in range(N_ZH):
                inverse = to_column(as_row(held[z * N_ZL + level, pl.ds(near * LINES, LINES), :]))
                if t == 0:
                    k = keys_ref[z * R : (z + 1) * R]
                else:
                    k = jnp.concatenate([far_ref[z * 8 + i, t - 1] for i in range(8)], axis=0)
                at = (t * N_ZH + z) * R
                both[at : at + R, 0:E] = k
                both[at : at + R, E : 2 * E] = (k.astype(jnp.float32) * inverse).astype(jnp.bfloat16)

    total = jnp.dot(own_ref[...], both[0:GATHERED], preferred_element_type=jnp.float32)
    total = total + jnp.dot(others_ref[...], both[GATHERED:], preferred_element_type=jnp.float32)
    column = to_column(as_row(mine_ref[pl.ds(piece * LINES, LINES), :]))
    out_ref[0] = column * total[:, 0:E] + total[:, E : 2 * E] - 2.0 * match_ref[...]


def finish_kernel(embed_ref, parts_ref, out_ref):
    x = embed_ref[...]
    inverse = lax.rsqrt(jnp.sum(x * x, axis=1, keepdims=True) + 1e-06)
    unit = x * inverse
    total = parts_ref[0]
    for i in range(1, N_X):
        total = total + parts_ref[i]
    direction = INVERSE_TAU * total
    out_ref[...] = inverse * (direction - unit * jnp.sum(unit * direction, axis=1, keepdims=True))


def f32(*shape):
    return jax.ShapeDtypeStruct(shape, jnp.float32)


def bf16(*shape):
    return jax.ShapeDtypeStruct(shape, jnp.bfloat16)


def exchange(value, axes):
    return lax.all_to_all(value, axes, 0, 0, tiled=True)


def call(kernel, out_shape, *args, specs=None, **more):
    several = isinstance(out_shape, tuple)
    return pl.pallas_call(
        kernel,
        out_shape=out_shape,
        in_specs=specs or [whole] * len(args),
        out_specs=more.pop("out_specs", (whole,) * len(out_shape) if several else whole),
        compiler_params=pltpu.CompilerParams(vmem_limit_bytes=VMEM),
        **more,
    )(*args)


def cost(keys):
    pairs = N_X * R * keys
    return pl.CostEstimate(flops=2 * pairs * E, bytes_accessed=2 * pairs, transcendentals=pairs)


def rows(width):
    return pl.BlockSpec((R, width), lambda g: (g, 0))


def leading(*shape):
    return pl.BlockSpec((1,) + shape, lambda g: (g,) + (0,) * len(shape))


def body(embed, partner, plan):
    far = ROUNDS * GATHERED
    with jax.named_scope("normalize"):
        rounded, sent = call(
            normalize_kernel, (bf16(R, E), bf16(N_X, SENT, E)), embed, partner.reshape(LINES, E)
        )
    with jax.named_scope("queries"):
        queries = exchange(sent, "x")
    with jax.named_scope("own"):
        keys = lax.all_gather(rounded, "zh", axis=0, tiled=True)
    with jax.named_scope("opponents"):
        chunks = exchange(keys.reshape(N_BLOCK, CHUNK, E), BLOCK)
        chosen = call(select_kernel, bf16(N_BLOCK, ROUNDS, CHUNK, E), plan, chunks, queries,
            specs=[smem, whole, pl.BlockSpec(memory_space=pl.ANY)])
        others = exchange(chosen, BLOCK)
    with jax.named_scope("own"):
        own_exps, match, own_sums = call(
            own_kernel,
            (bf16(N_X * R, GATHERED), f32(N_X * R, E), f32(N_X, 8, R)),
            queries,
            keys,
            specs=[leading(SENT, E), whole],
            out_specs=(rows(GATHERED), rows(E), leading(8, R)),
            grid=(N_X,),
            cost_estimate=cost(GATHERED),
        )
    with jax.named_scope("others"):
        exps, line = call(
            others_kernel,
            (bf16(N_X * R, far), f32(N_BLOCK, 16, E)),
            queries,
            others,
            own_sums,
            specs=[leading(SENT, E), whole, leading(8, R)],
            out_specs=(rows(far), pl.BlockSpec((N_BLOCK, 16, E), lambda g: (0, 0, 0))),
            grid=(N_X,),
            cost_estimate=cost(far),
        )
    with jax.named_scope("sums"):
        line = exchange(line, PLANE)
        level, mine, log_partition = call(
            sums_kernel,
            (bf16(N_ZH * N_ZL, 32, E), f32(16, E), f32(LINES, E)),
            line,
            scratch_shapes=[pltpu.VMEM((NEAR, 2, 16, E), jnp.float32)],
        )
        level = exchange(level, COLUMN)
        loss = jnp.sum(level[:, LOSS : LOSS + 3, 0].astype(jnp.float32)) / (N_BLOCK * BLOCK_ROWS)
    with jax.named_scope("direction"):
        parts = call(
            direction_kernel,
            f32(N_X, R, E),
            plan,
            own_exps,
            exps,
            keys,
            others,
            match,
            mine,
            level,
            specs=[smem, rows(GATHERED), rows(far), whole, whole, rows(E), whole, whole],
            scratch_shapes=[
                pltpu.VMEM((N_ZH * N_ZL, 32, E), jnp.float32),
                pltpu.VMEM((GATHERED + far, 2 * E), jnp.bfloat16),
            ],
            out_specs=leading(R, E),
            grid=(N_X,),
            cost_estimate=cost(GATHERED + far),
        )
        parts = exchange(parts, "x")
    with jax.named_scope("finish"):
        grad = call(finish_kernel, f32(R, E), embed, parts)
    return (grad, log_partition.reshape(R), loss)


def solution(mesh):
    split = Mesh(mesh.devices.reshape(SIZES), AXES)
    return jax.shard_map(
        body,
        mesh=split,
        in_specs=(P(AXES, None), P(AXES), P()),
        out_specs=(P(AXES, None), P(AXES), P()),
        check_vma=False,
    )
```

```python
import jax
import jax.numpy as jnp
import numpy as np
from jax import lax
from jax.experimental import pallas as pl
from jax.experimental.pallas import tpu as pltpu
from jax.sharding import Mesh
from jax.sharding import PartitionSpec as P

ROUNDS = 2
INVERSE_TAU = 10.0
SCALE = INVERSE_TAU * float(np.log2(np.e))

AXES = ("zl", "y", "c", "x", "zh")
SIZES = (4, 4, 2, 4, 4)
BLOCK = ("zl", "y", "c")
PLANE = ("y", "x", "c")
COLUMN = ("zh", "zl")

R = 384
E = 128
N_BLOCK = 32
N_X = 4
N_ZL = 4
N_ZH = 4
GATHERED = R * N_ZH
BLOCK_ROWS = GATHERED * N_X
CHUNK = GATHERED // N_BLOCK
SENT = R + 16
LINES = R // E
SLOT = LINES * N_X
NEAR = 8
LOSS = LINES * NEAR
VMEM = 12 * 1024 * 1024

whole = pl.BlockSpec(memory_space=pltpu.VMEM)
smem = pl.BlockSpec(memory_space=pltpu.SMEM)
anywhere = pl.BlockSpec(memory_space=pl.ANY)


def as_row(lines):
    return jnp.concatenate([lines[i : i + 1] for i in range(LINES)], axis=1)


def as_lines(row):
    return jnp.concatenate([row[0:1, i * E : (i + 1) * E] for i in range(LINES)], axis=0)


def to_column(row):
    return jnp.transpose(jnp.broadcast_to(row, (E, R)))


def widen(wide):
    return jnp.concatenate([wide] * LINES, axis=1)


def lane_sums(value):
    return jnp.sum(jnp.transpose(value), axis=0, keepdims=True)


def scores(q, k):
    return lax.dot_general(q, k, (((1,), (1,)), ((), ())), preferred_element_type=jnp.float32)


def fold(e):
    part = e[:, 0:E]
    for i in range(1, LINES):
        part = part + e[:, i * E : (i + 1) * E]
    return part


def far_keys(keys_ref, t, z):
    each = R // CHUNK
    return jnp.concatenate([keys_ref[z * each + i, t] for i in range(each)], axis=0)


def normalize_kernel(embed_ref, partner_ref, rounded_ref, sent_ref):
    x = embed_ref[...]
    inverse = lax.rsqrt(jnp.sum(x * x, axis=1, keepdims=True) + 1e-06)
    rounded = (x * inverse).astype(jnp.bfloat16)
    rounded_ref[...] = rounded
    index = partner_ref[...]
    high = index // 128
    low = index - high * 128
    both = jnp.concatenate([high, low, jnp.zeros((16 - 2 * LINES, E), jnp.int32)], axis=0)
    index = both.astype(jnp.float32).astype(jnp.bfloat16)
    for xp in range(N_X):
        sent_ref[xp, 0:R] = rounded
        sent_ref[xp, R:SENT] = index


def select_kernel(plan_ref, chunks_ref, queries_ref, out_ref):
    for b in range(N_BLOCK):
        for t in range(ROUNDS):
            out_ref[b, t] = chunks_ref[plan_ref[t, b]]


def own_kernel(queries_ref, keys_ref, exp_ref, match_ref, total_ref):
    x = lax.axis_index("x")
    zh = lax.axis_index("zh")
    lane = lax.broadcasted_iota(jnp.int32, (R, R), 1)
    itself = lax.broadcasted_iota(jnp.int32, (R, R), 0) - lane
    for piece in range(N_X):
        q = queries_ref[piece, 0:R]
        rows = slice(piece * R, (piece + 1) * R)
        index = queries_ref[piece, R:SENT].astype(jnp.float32)
        index = as_row(index[0:LINES]) * 128.0 + as_row(index[LINES : 2 * LINES])
        partner = widen(to_column(index)).astype(jnp.int32) - x * GATHERED - lane
        for z in range(N_ZH):
            k = keys_ref[z * R : (z + 1) * R]
            e = jnp.exp2(scores(q, k) * SCALE - SCALE)
            e = jnp.where(itself == (x - piece) * GATHERED + (z - zh) * R, 0.0, e)
            exp_ref[rows, z * R : (z + 1) * R] = e.astype(jnp.bfloat16)
            chosen = jnp.where(partner == z * R, 1.0, 0.0).astype(jnp.bfloat16)
            match = jnp.dot(chosen, k, preferred_element_type=jnp.float32)
            part = fold(e)
            if z > 0:
                match = match + match_ref[rows]
                part = part + total_ref[rows]
            match_ref[rows] = match
            total_ref[rows] = part


def others_kernel(queries_ref, keys_ref, match_ref, own_ref, exp_ref, line_ref, total):
    for t in range(ROUNDS):
        for z in range(N_ZH):
            k = far_keys(keys_ref, t, z)
            at = (t * N_ZH + z) * R
            for piece in range(N_X):
                rows = slice(piece * R, (piece + 1) * R)
                e = jnp.exp2(scores(queries_ref[piece, 0:R], k) * SCALE - SCALE)
                exp_ref[rows, at : at + R] = e.astype(jnp.bfloat16)
                total[rows] = fold(e) + (total[rows] if at > 0 else own_ref[rows])
    sums = lane_sums(total[...])
    lines = [sums[0:1, i * E : (i + 1) * E] for i in range(N_X * LINES)]
    positive = jnp.zeros((8, E), jnp.float32)
    for piece in range(N_X):
        match = match_ref[piece * R : (piece + 1) * R] * queries_ref[piece, 0:R].astype(jnp.float32)
        positive = positive + jnp.sum(match.reshape(R // 8, 8, E), axis=0)
    positive = jnp.sum(positive, axis=(0, 1), keepdims=True)
    lines = jnp.concatenate(lines + [jnp.broadcast_to(positive, (16 - SLOT, E))], axis=0)
    for i in range(N_BLOCK):
        line_ref[i] = lines


def sums_kernel(line_ref, level_ref, mine_ref, log_ref, held):
    near = lax.axis_index("y") * 2 + lax.axis_index("c")
    x = lax.axis_index("x")
    slot = lax.broadcasted_iota(jnp.int32, (16, E), 0)
    loss = jnp.zeros((16, E), jnp.float32)
    for i in range(NEAR):
        y, c = divmod(i, 2)
        part = line_ref[y * 8 + c]
        for j in range(1, N_X):
            part = part + line_ref[y * 8 + j * 2 + c]
        sums = jnp.where(slot < SLOT, part, 1.0)
        logs = INVERSE_TAU + jnp.log(sums)
        loss = loss + jnp.where(slot < SLOT, logs, 0.0)
        loss = loss - jnp.where(slot == SLOT, part * (INVERSE_TAU / E), 0.0)
        held[i, 0] = 1.0 / sums
        held[i, 1] = logs
    mine_ref[...] = held[near, 0]
    log_ref[...] = held[near, 1, pl.ds(x * LINES, LINES), :]
    level = [held[i, 0, pl.ds(x * LINES, LINES), :] for i in range(NEAR)]
    loss = jnp.broadcast_to(jnp.sum(loss, axis=(0, 1), keepdims=True), (1, E))
    for _ in range(3):
        level.append(loss.astype(jnp.bfloat16).astype(jnp.float32))
        loss = loss - level[-1]
    level.append(jnp.zeros((32 - LOSS - 3, E), jnp.float32))
    level = jnp.concatenate(level, axis=0).astype(jnp.bfloat16)
    for i in range(N_ZH * N_ZL):
        level_ref[i] = level


def direction_kernel(
    plan_ref, own_ref, others_ref, keys_ref, far_ref, match_ref, mine_ref, sums_ref, out_ref, held, both
):
    zl, y, c = (lax.axis_index(a) for a in BLOCK)
    here = (zl * 4 + y) * 2 + c
    held[...] = sums_ref[...].astype(jnp.float32)
    for t in range(ROUNDS + 1):
        other = here if t == 0 else plan_ref[t - 1, here]
        level = other // NEAR
        near = other - level * NEAR
        for z in range(N_ZH):
            inverse = to_column(as_row(held[z * N_ZL + level, pl.ds(near * LINES, LINES), :]))
            k = keys_ref[z * R : (z + 1) * R] if t == 0 else far_keys(far_ref, t - 1, z)
            at = (t * N_ZH + z) * R
            both[at : at + R, 0:E] = k
            both[at : at + R, E : 2 * E] = (k.astype(jnp.float32) * inverse).astype(jnp.bfloat16)
    for piece in range(N_X):
        rows = slice(piece * R, (piece + 1) * R)
        total = jnp.dot(own_ref[rows], both[0:GATHERED], preferred_element_type=jnp.float32)
        total = total + jnp.dot(others_ref[rows], both[GATHERED:], preferred_element_type=jnp.float32)
        column = to_column(as_row(mine_ref[piece * LINES : (piece + 1) * LINES, :]))
        out_ref[piece] = column * total[:, 0:E] + total[:, E : 2 * E] - 2.0 * match_ref[rows]


def finish_kernel(embed_ref, parts_ref, out_ref):
    x = embed_ref[...]
    inverse = lax.rsqrt(jnp.sum(x * x, axis=1, keepdims=True) + 1e-06)
    unit = x * inverse
    total = parts_ref[0]
    for i in range(1, N_X):
        total = total + parts_ref[i]
    direction = INVERSE_TAU * total
    out_ref[...] = inverse * (direction - unit * jnp.sum(unit * direction, axis=1, keepdims=True))


def f32(*shape):
    return jax.ShapeDtypeStruct(shape, jnp.float32)


def bf16(*shape):
    return jax.ShapeDtypeStruct(shape, jnp.bfloat16)


def exchange(value, axes):
    return lax.all_to_all(value, axes, 0, 0, tiled=True)


def call(kernel, out_shape, *args, specs=None, **more):
    return pl.pallas_call(
        kernel,
        out_shape=out_shape,
        in_specs=specs or [whole] * len(args),
        out_specs=(whole,) * len(out_shape) if isinstance(out_shape, tuple) else whole,
        compiler_params=pltpu.CompilerParams(vmem_limit_bytes=VMEM),
        **more,
    )(*args)


def cost(keys):
    pairs = N_X * R * keys
    return pl.CostEstimate(flops=2 * pairs * E, bytes_accessed=2 * pairs, transcendentals=pairs)


def body(embed, partner, plan):
    far = ROUNDS * GATHERED
    with jax.named_scope("normalize"):
        rounded, sent = call(
            normalize_kernel, (bf16(R, E), bf16(N_X, SENT, E)), embed, partner.reshape(LINES, E)
        )
    with jax.named_scope("queries"):
        queries = exchange(sent, "x")
    with jax.named_scope("own"):
        keys = lax.all_gather(rounded, "zh", axis=0, tiled=True)
    with jax.named_scope("opponents"):
        chunks = exchange(keys.reshape(N_BLOCK, CHUNK, E), BLOCK)
        chosen = call(select_kernel, bf16(N_BLOCK, ROUNDS, CHUNK, E), plan, chunks, queries,
            specs=[smem, whole, anywhere])
        others = exchange(chosen, BLOCK)
    with jax.named_scope("own"):
        own_exps, match, total = call(
            own_kernel,
            (bf16(N_X * R, GATHERED), f32(N_X * R, E), f32(N_X * R, E)),
            queries,
            keys,
            cost_estimate=cost(GATHERED),
        )
    with jax.named_scope("others"):
        exps, line = call(
            others_kernel,
            (bf16(N_X * R, far), f32(N_BLOCK, 16, E)),
            queries,
            others,
            match,
            total,
            scratch_shapes=[pltpu.VMEM((N_X * R, E), jnp.float32)],
            cost_estimate=cost(far),
        )
    with jax.named_scope("sums"):
        line = exchange(line, PLANE)
        level, mine, log_partition = call(
            sums_kernel,
            (bf16(N_ZH * N_ZL, 32, E), f32(16, E), f32(LINES, E)),
            line,
            scratch_shapes=[pltpu.VMEM((NEAR, 2, 16, E), jnp.float32)],
        )
        level = exchange(level, COLUMN)
        loss = jnp.sum(level[:, LOSS : LOSS + 3, 0].astype(jnp.float32)) / (N_BLOCK * BLOCK_ROWS)
    with jax.named_scope("direction"):
        parts = call(
            direction_kernel,
            f32(N_X, R, E),
            plan,
            own_exps,
            exps,
            keys,
            others,
            match,
            mine,
            level,
            specs=[smem] + [whole] * 7,
            scratch_shapes=[
                pltpu.VMEM((N_ZH * N_ZL, 32, E), jnp.float32),
                pltpu.VMEM((GATHERED + far, 2 * E), jnp.bfloat16),
            ],
            cost_estimate=cost(GATHERED + far),
        )
        parts = exchange(parts, "x")
    with jax.named_scope("finish"):
        grad = call(finish_kernel, f32(R, E), embed, parts)
    return (grad, log_partition.reshape(R), loss)


def solution(mesh):
    split = Mesh(mesh.devices.reshape(SIZES), AXES)
    return jax.shard_map(
        body,
        mesh=split,
        in_specs=(P(AXES, None), P(AXES), P()),
        out_specs=(P(AXES, None), P(AXES), P()),
        check_vma=False,
    )
```

```python
import jax
import jax.numpy as jnp
import numpy as np
from jax import lax
from jax.experimental import pallas as pl
from jax.experimental.pallas import tpu as pltpu
from jax.sharding import Mesh
from jax.sharding import PartitionSpec as P

ROUNDS = 2
INVERSE_TAU = 10.0
SCALE = INVERSE_TAU * float(np.log2(np.e))

AXES = ("zl", "y", "c", "x", "zh")
SIZES = (4, 4, 2, 4, 4)
BLOCK = ("zl", "y", "c")
PLANE = ("y", "x", "c")
COLUMN = ("zh", "zl")

R = 384
E = 128
N_BLOCK = 32
N_X = 4
N_ZL = 4
N_ZH = 4
GATHERED = R * N_ZH
BLOCK_ROWS = GATHERED * N_X
CHUNK = GATHERED // N_BLOCK
SENT = R + 16
LINES = R // E
SLOT = LINES * N_X
NEAR = 8
LOSS = LINES * NEAR
VMEM = 12 * 1024 * 1024

whole = pl.BlockSpec(memory_space=pltpu.VMEM)
smem = pl.BlockSpec(memory_space=pltpu.SMEM)


def as_row(lines):
    return jnp.concatenate([lines[i : i + 1] for i in range(LINES)], axis=1)


def as_lines(row):
    return jnp.concatenate([row[0:1, i * E : (i + 1) * E] for i in range(LINES)], axis=0)


def to_column(row):
    return jnp.transpose(jnp.broadcast_to(row, (E, R)))


def widen(wide):
    return jnp.concatenate([wide] * LINES, axis=1)


def lane_sums(value):
    return jnp.sum(jnp.transpose(value), axis=0, keepdims=True)


def scores(q, k):
    return lax.dot_general(q, k, (((1,), (1,)), ((), ())), preferred_element_type=jnp.float32)


def fold(e):
    part = e[:, 0:E]
    for i in range(1, LINES):
        part = part + e[:, i * E : (i + 1) * E]
    return part


def far_keys(keys_ref, t, z):
    each = R // CHUNK
    return jnp.concatenate([keys_ref[z * each + i, t] for i in range(each)], axis=0)


def normalize_kernel(embed_ref, partner_ref, rounded_ref, sent_ref):
    x = embed_ref[...]
    inverse = lax.rsqrt(jnp.sum(x * x, axis=1, keepdims=True) + 1e-06)
    rounded = (x * inverse).astype(jnp.bfloat16)
    rounded_ref[...] = rounded
    index = partner_ref[...]
    high = index // 128
    low = index - high * 128
    both = jnp.concatenate([high, low, jnp.zeros((16 - 2 * LINES, E), jnp.int32)], axis=0)
    index = both.astype(jnp.float32).astype(jnp.bfloat16)
    sent_ref[0:R] = rounded
    sent_ref[R:SENT] = index


def select_kernel(plan_ref, chunks_ref, out_ref):
    for b in range(N_BLOCK):
        for t in range(ROUNDS):
            out_ref[b, t] = chunks_ref[plan_ref[t, b]]


def own_kernel(queries_ref, keys_ref, exp_ref, match_ref, total_ref, positive_ref):
    x = lax.axis_index("x")
    zh = lax.axis_index("zh")
    lane = lax.broadcasted_iota(jnp.int32, (R, R), 1)
    itself = lax.broadcasted_iota(jnp.int32, (R, R), 0) - lane
    positive = jnp.zeros((8, E), jnp.float32)
    for piece in range(N_X):
        q = queries_ref[piece, 0:R]
        rows = slice(piece * R, (piece + 1) * R)
        index = queries_ref[piece, R:SENT].astype(jnp.float32)
        index = as_row(index[0:LINES]) * 128.0 + as_row(index[LINES : 2 * LINES])
        partner = widen(to_column(index)).astype(jnp.int32) - x * GATHERED - lane
        for z in range(N_ZH):
            k = keys_ref[z * R : (z + 1) * R]
            e = jnp.exp2(scores(q, k) * SCALE - SCALE)
            e = jnp.where(itself == (x - piece) * GATHERED + (z - zh) * R, 0.0, e)
            exp_ref[rows, z * R : (z + 1) * R] = e.astype(jnp.bfloat16)
            chosen = jnp.where(partner == z * R, 1.0, 0.0).astype(jnp.bfloat16)
            match = jnp.dot(chosen, k, preferred_element_type=jnp.float32)
            part = fold(e)
            if z > 0:
                match = match + match_ref[rows]
                part = part + total_ref[rows]
            match_ref[rows] = match
            total_ref[rows] = part
        match = match * q.astype(jnp.float32)
        positive = positive + jnp.sum(match.reshape(R // 8, 8, E), axis=0)
    positive_ref[...] = jnp.broadcast_to(jnp.sum(positive, axis=(0, 1), keepdims=True), (8, E))


def others_kernel(queries_ref, keys_ref, positive_ref, own_ref, exp_ref, line_ref, total):
    for t in range(ROUNDS):
        for z in range(N_ZH):
            k = far_keys(keys_ref, t, z)
            at = (t * N_ZH + z) * R
            for piece in range(N_X):
                rows = slice(piece * R, (piece + 1) * R)
                e = jnp.exp2(scores(queries_ref[piece, 0:R], k) * SCALE - SCALE)
                exp_ref[rows, at : at + R] = e.astype(jnp.bfloat16)
                total[rows] = fold(e) + (total[rows] if at > 0 else own_ref[rows])
    sums = lane_sums(total[...])
    lines = [sums[0:1, i * E : (i + 1) * E] for i in range(N_X * LINES)]
    lines = jnp.concatenate(lines + [positive_ref[0 : 16 - SLOT]], axis=0)
    for i in range(N_BLOCK):
        line_ref[i] = lines


def sums_kernel(line_ref, level_ref, mine_ref, log_ref, held):
    near = lax.axis_index("y") * 2 + lax.axis_index("c")
    x = lax.axis_index("x")
    slot = lax.broadcasted_iota(jnp.int32, (16, E), 0)
    loss = jnp.zeros((16, E), jnp.float32)
    for i in range(NEAR):
        y, c = divmod(i, 2)
        part = line_ref[y * 8 + c]
        for j in range(1, N_X):
            part = part + line_ref[y * 8 + j * 2 + c]
        sums = jnp.where(slot < SLOT, part, 1.0)
        logs = INVERSE_TAU + jnp.log(sums)
        loss = loss + jnp.where(slot < SLOT, logs, 0.0)
        loss = loss - jnp.where(slot == SLOT, part * (INVERSE_TAU / E), 0.0)
        held[i, 0] = 1.0 / sums
        held[i, 1] = logs
    mine_ref[...] = held[near, 0]
    log_ref[...] = held[near, 1, pl.ds(x * LINES, LINES), :]
    level = [held[i, 0, pl.ds(x * LINES, LINES), :] for i in range(NEAR)]
    loss = jnp.broadcast_to(jnp.sum(loss, axis=(0, 1), keepdims=True), (1, E))
    for _ in range(3):
        level.append(loss.astype(jnp.bfloat16).astype(jnp.float32))
        loss = loss - level[-1]
    level.append(jnp.zeros((32 - LOSS - 3, E), jnp.float32))
    level = jnp.concatenate(level, axis=0).astype(jnp.bfloat16)
    for i in range(N_ZH * N_ZL):
        level_ref[i] = level


def direction_kernel(
    plan_ref, own_ref, others_ref, keys_ref, far_ref, match_ref, mine_ref, sums_ref, out_ref, loss_ref, held, both
):
    zl, y, c = (lax.axis_index(a) for a in BLOCK)
    here = (zl * 4 + y) * 2 + c
    held[...] = sums_ref[...].astype(jnp.float32)
    loss = held[0, LOSS : LOSS + 3, :]
    for i in range(1, N_ZH * N_ZL):
        loss = loss + held[i, LOSS : LOSS + 3, :]
    loss_ref[...] = jnp.sum(loss, axis=0, keepdims=True)[:, 0:1] / (N_BLOCK * BLOCK_ROWS)
    for t in range(ROUNDS + 1):
        other = here if t == 0 else plan_ref[t - 1, here]
        level = other // NEAR
        near = other - level * NEAR
        for z in range(N_ZH):
            inverse = to_column(as_row(held[z * N_ZL + level, pl.ds(near * LINES, LINES), :]))
            k = keys_ref[z * R : (z + 1) * R] if t == 0 else far_keys(far_ref, t - 1, z)
            at = (t * N_ZH + z) * R
            both[at : at + R, 0:E] = k
            both[at : at + R, E : 2 * E] = (k.astype(jnp.float32) * inverse).astype(jnp.bfloat16)
    for piece in range(N_X):
        rows = slice(piece * R, (piece + 1) * R)
        total = jnp.dot(own_ref[rows], both[0:GATHERED], preferred_element_type=jnp.float32)
        total = total + jnp.dot(others_ref[rows], both[GATHERED:], preferred_element_type=jnp.float32)
        column = to_column(as_row(mine_ref[piece * LINES : (piece + 1) * LINES, :]))
        out_ref[piece] = column * total[:, 0:E] + total[:, E : 2 * E] - 2.0 * match_ref[rows]


def finish_kernel(embed_ref, parts_ref, out_ref):
    x = embed_ref[...]
    inverse = lax.rsqrt(jnp.sum(x * x, axis=1, keepdims=True) + 1e-06)
    unit = x * inverse
    total = parts_ref[0]
    for i in range(1, N_X):
        total = total + parts_ref[i]
    direction = INVERSE_TAU * total
    out_ref[...] = inverse * (direction - unit * jnp.sum(unit * direction, axis=1, keepdims=True))


def f32(*shape):
    return jax.ShapeDtypeStruct(shape, jnp.float32)


def bf16(*shape):
    return jax.ShapeDtypeStruct(shape, jnp.bfloat16)


def exchange(value, axes):
    return lax.all_to_all(value, axes, 0, 0, tiled=True)


def call(kernel, out_shape, *args, specs=None, **more):
    return pl.pallas_call(
        kernel,
        out_shape=out_shape,
        in_specs=specs or [whole] * len(args),
        out_specs=(whole,) * len(out_shape) if isinstance(out_shape, tuple) else whole,
        compiler_params=pltpu.CompilerParams(vmem_limit_bytes=VMEM),
        **more,
    )(*args)


def cost(keys):
    pairs = N_X * R * keys
    return pl.CostEstimate(flops=2 * pairs * E, bytes_accessed=2 * pairs, transcendentals=pairs)


def body(embed, partner, plan):
    far = ROUNDS * GATHERED
    with jax.named_scope("normalize"):
        rounded, sent = pl.pallas_call(
            normalize_kernel,
            grid=(1,),
            out_shape=(bf16(R, E), bf16(SENT, E)),
            in_specs=[pl.BlockSpec((R, E), lambda g: (0, 0)), pl.BlockSpec((LINES, E), lambda g: (0, 0))],
            out_specs=(whole, whole),
        )(embed, partner.reshape(LINES, E))
    with jax.named_scope("own"):
        keys = lax.all_gather(rounded, "zh", axis=0, tiled=True)
    with jax.named_scope("opponents"):
        chunks = exchange(keys.reshape(N_BLOCK, CHUNK, E), BLOCK)
        chosen = call(select_kernel, bf16(N_BLOCK, ROUNDS, CHUNK, E), plan, chunks, specs=[smem, whole])
        others = exchange(chosen, BLOCK)
    with jax.named_scope("queries"):
        queries = lax.all_gather(sent, "x", axis=0)
    with jax.named_scope("own"):
        own_exps, match, total, positive = call(
            own_kernel,
            (bf16(N_X * R, GATHERED), f32(N_X * R, E), f32(N_X * R, E), f32(8, E)),
            queries,
            keys,
            cost_estimate=cost(GATHERED),
        )
    with jax.named_scope("others"):
        exps, line = call(
            others_kernel,
            (bf16(N_X * R, far), f32(N_BLOCK, 16, E)),
            queries,
            others,
            positive,
            total,
            scratch_shapes=[pltpu.VMEM((N_X * R, E), jnp.float32)],
            cost_estimate=cost(far),
        )
    with jax.named_scope("sums"):
        line = exchange(line, PLANE)
        level, mine, log_partition = call(
            sums_kernel,
            (bf16(N_ZH * N_ZL, 32, E), f32(16, E), f32(LINES, E)),
            line,
            scratch_shapes=[pltpu.VMEM((NEAR, 2, 16, E), jnp.float32)],
        )
        level = exchange(level, COLUMN)
    with jax.named_scope("direction"):
        parts, loss = call(
            direction_kernel,
            (f32(N_X, R, E), f32(1, 1)),
            plan,
            own_exps,
            exps,
            keys,
            others,
            match,
            mine,
            level,
            specs=[smem] + [whole] * 7,
            scratch_shapes=[
                pltpu.VMEM((N_ZH * N_ZL, 32, E), jnp.float32),
                pltpu.VMEM((GATHERED + far, 2 * E), jnp.bfloat16),
            ],
            cost_estimate=cost(GATHERED + far),
        )
        parts = exchange(parts, "x")
    with jax.named_scope("finish"):
        grad = call(finish_kernel, f32(R, E), embed, parts)
    return (grad, log_partition.reshape(R), loss.reshape(()))


def solution(mesh):
    split = Mesh(mesh.devices.reshape(SIZES), AXES)
    return jax.shard_map(
        body,
        mesh=split,
        in_specs=(P(AXES, None), P(AXES), P()),
        out_specs=(P(AXES, None), P(AXES), P()),
        check_vma=False,
    )
```

```python
import jax
import jax.numpy as jnp
import numpy as np
from jax import lax
from jax.experimental import pallas as pl
from jax.experimental.pallas import tpu as pltpu
from jax.sharding import Mesh
from jax.sharding import PartitionSpec as P

ROUNDS = 2
INVERSE_TAU = 10.0
SCALE = INVERSE_TAU * float(np.log2(np.e))

AXES = ("zl", "y", "c", "x", "zh")
SIZES = (4, 4, 2, 4, 4)
BLOCK = ("zl", "y", "c")
PLANE = ("c", "y", "x")
COLUMN = ("zl", "zh")

R = 384
E = 128
N_BLOCK = 32
N_X = 4
N_ZL = 4
N_ZH = 4
GATHERED = R * N_ZH
BLOCK_ROWS = GATHERED * N_X
CHUNK = GATHERED // N_BLOCK
SENT = R + 16
LINES = R // E
SLOT = LINES * N_X
NEAR = 8
LOSS = LINES * NEAR
VMEM = 12 * 1024 * 1024

whole = pl.BlockSpec(memory_space=pltpu.VMEM)
smem = pl.BlockSpec(memory_space=pltpu.SMEM)


def as_row(lines):
    return jnp.concatenate([lines[i : i + 1] for i in range(LINES)], axis=1)


def as_lines(row):
    return jnp.concatenate([row[0:1, i * E : (i + 1) * E] for i in range(LINES)], axis=0)


def to_column(row):
    return jnp.transpose(jnp.broadcast_to(row, (E, R)))


def widen(wide):
    return jnp.concatenate([wide] * LINES, axis=1)


def lane_sums(value):
    return jnp.sum(jnp.transpose(value), axis=0, keepdims=True)


def scores(q, k):
    return lax.dot_general(q, k, (((1,), (1,)), ((), ())), preferred_element_type=jnp.float32)


def fold(e):
    part = e[:, 0:E]
    for i in range(1, LINES):
        part = part + e[:, i * E : (i + 1) * E]
    return part


def far_keys(keys_ref, t, z):
    each = R // CHUNK
    return jnp.concatenate([keys_ref[z * each + i, t] for i in range(each)], axis=0)


def normalize_kernel(embed_ref, partner_ref, rounded_ref, sent_ref):
    x = embed_ref[...]
    inverse = lax.rsqrt(jnp.sum(x * x, axis=1, keepdims=True) + 1e-06)
    rounded = (x * inverse).astype(jnp.bfloat16)
    rounded_ref[...] = rounded
    index = partner_ref[...]
    high = index // 128
    low = index - high * 128
    both = jnp.concatenate([high, low, jnp.zeros((16 - 2 * LINES, E), jnp.int32)], axis=0)
    index = both.astype(jnp.float32).astype(jnp.bfloat16)
    sent_ref[0:R] = rounded
    sent_ref[R:SENT] = index


def select_kernel(plan_ref, chunks_ref, out_ref):
    for start in range(0, N_BLOCK, 8):
        several = range(start, start + 8)
        taken = [[chunks_ref[plan_ref[t, b]] for t in range(ROUNDS)] for b in several]
        for b in several:
            for t in range(ROUNDS):
                out_ref[b, t] = taken[b - start][t]


def own_kernel(queries_ref, keys_ref, exp_ref, match_ref, total_ref, positive_ref):
    x = lax.axis_index("x")
    zh = lax.axis_index("zh")
    lane = lax.broadcasted_iota(jnp.int32, (R, R), 1)
    itself = lax.broadcasted_iota(jnp.int32, (R, R), 0) - lane
    positive = jnp.zeros((8, E), jnp.float32)
    for piece in range(N_X):
        q = queries_ref[piece, 0:R]
        rows = slice(piece * R, (piece + 1) * R)
        index = queries_ref[piece, R:SENT].astype(jnp.float32)
        index = as_row(index[0:LINES]) * 128.0 + as_row(index[LINES : 2 * LINES])
        partner = widen(to_column(index)).astype(jnp.int32) - x * GATHERED - lane
        for z in range(N_ZH):
            k = keys_ref[z * R : (z + 1) * R]
            e = jnp.exp2(scores(q, k) * SCALE)
            e = jnp.where(itself == (x - piece) * GATHERED + (z - zh) * R, 0.0, e)
            exp_ref[rows, z * R : (z + 1) * R] = e.astype(jnp.bfloat16)
            chosen = jnp.where(partner == z * R, 1.0, 0.0).astype(jnp.bfloat16)
            match = jnp.dot(chosen, k, preferred_element_type=jnp.float32)
            part = fold(e)
            if z > 0:
                match = match + match_ref[rows]
                part = part + total_ref[rows]
            match_ref[rows] = match
            total_ref[rows] = part
        match = match * q.astype(jnp.float32)
        positive = positive + jnp.sum(match.reshape(R // 8, 8, E), axis=0)
    positive_ref[...] = jnp.broadcast_to(jnp.sum(positive, axis=(0, 1), keepdims=True), (8, E))


def others_kernel(queries_ref, keys_ref, positive_ref, own_ref, exp_ref, line_ref, total):
    for t in range(ROUNDS):
        for z in range(N_ZH):
            k = far_keys(keys_ref, t, z)
            at = (t * N_ZH + z) * R
            for piece in range(N_X):
                rows = slice(piece * R, (piece + 1) * R)
                e = jnp.exp2(scores(queries_ref[piece, 0:R], k) * SCALE)
                exp_ref[rows, at : at + R] = e.astype(jnp.bfloat16)
                total[rows] = fold(e) + (total[rows] if at > 0 else own_ref[rows])
    sums = lane_sums(total[...])
    lines = [sums[0:1, i * E : (i + 1) * E] for i in range(N_X * LINES)]
    lines = jnp.concatenate(lines + [positive_ref[0 : 16 - SLOT]], axis=0)
    for i in range(N_BLOCK):
        line_ref[i] = lines


def sums_kernel(line_ref, level_ref, mine_ref, log_ref, held):
    near = lax.axis_index("y") * 2 + lax.axis_index("c")
    x = lax.axis_index("x")
    slot = lax.broadcasted_iota(jnp.int32, (16, E), 0)
    loss = jnp.zeros((16, E), jnp.float32)
    for i in range(NEAR):
        y, c = divmod(i, 2)
        at = (c * 4 + y) * N_X
        part = line_ref[at]
        for j in range(1, N_X):
            part = part + line_ref[at + j]
        sums = jnp.where(slot < SLOT, part, 1.0)
        logs = jnp.log(sums)
        loss = loss + jnp.where(slot < SLOT, logs, 0.0)
        loss = loss - jnp.where(slot == SLOT, part * (INVERSE_TAU / E), 0.0)
        held[i, 0] = 1.0 / sums
        held[i, 1] = logs
    mine_ref[...] = held[near, 0]
    log_ref[...] = held[near, 1, pl.ds(x * LINES, LINES), :]
    level = [held[i, 0, pl.ds(x * LINES, LINES), :] for i in range(NEAR)]
    loss = jnp.broadcast_to(jnp.sum(loss, axis=(0, 1), keepdims=True), (1, E))
    for _ in range(3):
        level.append(loss.astype(jnp.bfloat16).astype(jnp.float32))
        loss = loss - level[-1]
    level.append(jnp.zeros((32 - LOSS - 3, E), jnp.float32))
    level = jnp.concatenate(level, axis=0).astype(jnp.bfloat16)
    for i in range(N_ZH * N_ZL):
        level_ref[i] = level


def direction_kernel(
    plan_ref, own_ref, others_ref, keys_ref, far_ref, match_ref, mine_ref, sums_ref, out_ref, loss_ref, held, both
):
    zl, y, c = (lax.axis_index(a) for a in BLOCK)
    here = (zl * 4 + y) * 2 + c
    held[...] = sums_ref[...].astype(jnp.float32)
    loss = held[0, LOSS : LOSS + 3, :]
    for i in range(1, N_ZH * N_ZL):
        loss = loss + held[i, LOSS : LOSS + 3, :]
    loss_ref[...] = jnp.sum(loss, axis=0, keepdims=True)[:, 0:1] / (N_BLOCK * BLOCK_ROWS)
    for t in range(ROUNDS + 1):
        other = here if t == 0 else plan_ref[t - 1, here]
        level = other // NEAR
        near = other - level * NEAR
        for z in range(N_ZH):
            inverse = to_column(as_row(held[level * N_ZH + z, pl.ds(near * LINES, LINES), :]))
            k = keys_ref[z * R : (z + 1) * R] if t == 0 else far_keys(far_ref, t - 1, z)
            at = (t * N_ZH + z) * R
            both[at : at + R, 0:E] = k
            both[at : at + R, E : 2 * E] = (k.astype(jnp.float32) * inverse).astype(jnp.bfloat16)
    for piece in range(N_X):
        rows = slice(piece * R, (piece + 1) * R)
        total = jnp.dot(own_ref[rows], both[0:GATHERED], preferred_element_type=jnp.float32)
        total = total + jnp.dot(others_ref[rows], both[GATHERED:], preferred_element_type=jnp.float32)
        column = to_column(as_row(mine_ref[piece * LINES : (piece + 1) * LINES, :]))
        out_ref[piece] = column * total[:, 0:E] + total[:, E : 2 * E] - 2.0 * match_ref[rows]


def finish_kernel(embed_ref, parts_ref, out_ref):
    x = embed_ref[...]
    inverse = lax.rsqrt(jnp.sum(x * x, axis=1, keepdims=True) + 1e-06)
    unit = x * inverse
    total = parts_ref[0]
    for i in range(1, N_X):
        total = total + parts_ref[i]
    direction = INVERSE_TAU * total
    out_ref[...] = inverse * (direction - unit * jnp.sum(unit * direction, axis=1, keepdims=True))


def f32(*shape):
    return jax.ShapeDtypeStruct(shape, jnp.float32)


def bf16(*shape):
    return jax.ShapeDtypeStruct(shape, jnp.bfloat16)


def exchange(value, axes):
    return lax.all_to_all(value, axes, 0, 0, tiled=True)


def call(kernel, out_shape, *args, specs=None, **more):
    return pl.pallas_call(
        kernel,
        out_shape=out_shape,
        in_specs=specs or [whole] * len(args),
        out_specs=(whole,) * len(out_shape) if isinstance(out_shape, tuple) else whole,
        compiler_params=pltpu.CompilerParams(vmem_limit_bytes=VMEM),
        **more,
    )(*args)


def cost(keys):
    pairs = N_X * R * keys
    return pl.CostEstimate(flops=2 * pairs * E, bytes_accessed=2 * pairs, transcendentals=pairs)


def body(embed, partner, plan):
    far = ROUNDS * GATHERED
    with jax.named_scope("normalize"):
        rounded, sent = pl.pallas_call(
            normalize_kernel,
            grid=(1,),
            out_shape=(bf16(R, E), bf16(SENT, E)),
            in_specs=[pl.BlockSpec((R, E), lambda g: (0, 0)), pl.BlockSpec((LINES, E), lambda g: (0, 0))],
            out_specs=(whole, whole),
        )(embed, partner.reshape(LINES, E))
    with jax.named_scope("own"):
        keys = lax.all_gather(rounded, "zh", axis=0, tiled=True)
    with jax.named_scope("opponents"):
        chunks = exchange(keys.reshape(N_BLOCK, CHUNK, E), BLOCK)
        chosen = call(select_kernel, bf16(N_BLOCK, ROUNDS, CHUNK, E), plan, chunks, specs=[smem, whole])
        others = exchange(chosen, BLOCK)
    with jax.named_scope("queries"):
        queries = lax.all_gather(sent, "x", axis=0)
    with jax.named_scope("own"):
        own_exps, match, total, positive = call(
            own_kernel,
            (bf16(N_X * R, GATHERED), f32(N_X * R, E), f32(N_X * R, E), f32(8, E)),
            queries,
            keys,
            cost_estimate=cost(GATHERED),
        )
    with jax.named_scope("others"):
        exps, line = call(
            others_kernel,
            (bf16(N_X * R, far), f32(N_BLOCK, 16, E)),
            queries,
            others,
            positive,
            total,
            scratch_shapes=[pltpu.VMEM((N_X * R, E), jnp.float32)],
            cost_estimate=cost(far),
        )
    with jax.named_scope("sums"):
        line = exchange(line, PLANE)
        level, mine, log_partition = call(
            sums_kernel,
            (bf16(N_ZH * N_ZL, 32, E), f32(16, E), f32(LINES, E)),
            line,
            scratch_shapes=[pltpu.VMEM((NEAR, 2, 16, E), jnp.float32)],
        )
        level = exchange(level, COLUMN)
    with jax.named_scope("direction"):
        parts, loss = call(
            direction_kernel,
            (f32(N_X, R, E), f32(1, 1)),
            plan,
            own_exps,
            exps,
            keys,
            others,
            match,
            mine,
            level,
            specs=[smem] + [whole] * 7,
            scratch_shapes=[
                pltpu.VMEM((N_ZH * N_ZL, 32, E), jnp.float32),
                pltpu.VMEM((GATHERED + far, 2 * E), jnp.bfloat16),
            ],
            cost_estimate=cost(GATHERED + far),
        )
        parts = exchange(parts, "x")
    with jax.named_scope("finish"):
        grad = call(finish_kernel, f32(R, E), embed, parts)
    return (grad, log_partition.reshape(R), loss.reshape(()))


def solution(mesh):
    split = Mesh(mesh.devices.reshape(SIZES), AXES)
    return jax.shard_map(
        body,
        mesh=split,
        in_specs=(P(AXES, None), P(AXES), P()),
        out_specs=(P(AXES, None), P(AXES), P()),
        check_vma=False,
    )
```

```python
import jax
import jax.numpy as jnp
import numpy as np
from jax import lax
from jax.experimental import pallas as pl
from jax.experimental.pallas import tpu as pltpu
from jax.sharding import Mesh
from jax.sharding import PartitionSpec as P

ROUNDS = 2
INVERSE_TAU = 10.0
SCALE = INVERSE_TAU * float(np.log2(np.e))

AXES = ("zu", "zl", "y", "c", "x", "zh")
SIZES = (2, 2, 4, 2, 4, 4)
BLOCK = ("zu", "zl", "y", "c")
HALF = ("zl", "y", "c")
PLANE = ("c", "y", "x")
COLUMN = ("zu", "zl", "zh")

R = 384
E = 128
N_BLOCK = 32
N_X = 4
N_ZL = 4
N_ZH = 4
GATHERED = R * N_ZH
BLOCK_ROWS = GATHERED * N_X
N_HALF = N_BLOCK // 2
CHUNK = GATHERED // N_HALF
SENT = R + 16
LINES = R // E
SLOT = LINES * N_X
NEAR = 8
LOSS = LINES * NEAR
VMEM = 5 * 1024 * 1024

whole = pl.BlockSpec(memory_space=pltpu.VMEM)
smem = pl.BlockSpec(memory_space=pltpu.SMEM)
anywhere = pl.BlockSpec(memory_space=pl.ANY)


def as_row(lines):
    return jnp.concatenate([lines[i : i + 1] for i in range(LINES)], axis=1)


def as_lines(row):
    return jnp.concatenate([row[0:1, i * E : (i + 1) * E] for i in range(LINES)], axis=0)


def to_column(row):
    return jnp.transpose(jnp.broadcast_to(row, (E, R)))


def widen(wide):
    return jnp.concatenate([wide] * LINES, axis=1)


def lane_sums(value):
    return jnp.sum(jnp.transpose(value), axis=0, keepdims=True)


def scores(q, k):
    return lax.dot_general(q, k, (((1,), (1,)), ((), ())), preferred_element_type=jnp.float32)


def fold(e):
    part = e[:, 0:E]
    for i in range(1, LINES):
        part = part + e[:, i * E : (i + 1) * E]
    return part


def far_keys(keys_ref, t, z):
    each = R // CHUNK
    return jnp.concatenate([keys_ref[z * each + i, t] for i in range(each)], axis=0)


def normalize_kernel(embed_ref, partner_ref, plan_ref, rounded_ref, sent_ref, copy_ref):
    x = embed_ref[...]
    inverse = lax.rsqrt(jnp.sum(x * x, axis=1, keepdims=True) + 1e-06)
    rounded = (x * inverse).astype(jnp.bfloat16)
    rounded_ref[...] = rounded
    index = partner_ref[...]
    high = index // 128
    low = index - high * 128
    both = jnp.concatenate([high, low, jnp.zeros((16 - 2 * LINES, E), jnp.int32)], axis=0)
    index = both.astype(jnp.float32).astype(jnp.bfloat16)
    sent_ref[0:R] = rounded
    sent_ref[R:SENT] = index
    copy_ref[...] = plan_ref[...]


def select_kernel(plan_ref, chunks_ref, queries_ref, out_ref):
    first = lax.axis_index("zu") * N_HALF
    for start in range(0, N_HALF, 4):
        several = range(start, start + 4)
        taken = [[chunks_ref[plan_ref[t, first + b]] for t in range(ROUNDS)] for b in several]
        for b in several:
            for t in range(ROUNDS):
                out_ref[b, t] = taken[b - start][t]


def own_kernel(queries_ref, keys_ref, exp_ref, match_ref, sums_ref):
    x = lax.axis_index("x")
    zh = lax.axis_index("zh")
    lane = lax.broadcasted_iota(jnp.int32, (R, R), 1)
    itself = lax.broadcasted_iota(jnp.int32, (R, R), 0) - lane
    positive = jnp.zeros((8, E), jnp.float32)
    lines = []
    for piece in range(N_X):
        q = queries_ref[piece, 0:R]
        rows = slice(piece * R, (piece + 1) * R)
        index = queries_ref[piece, R:SENT].astype(jnp.float32)
        index = as_row(index[0:LINES]) * 128.0 + as_row(index[LINES : 2 * LINES])
        partner = widen(to_column(index)).astype(jnp.int32) - x * GATHERED - lane
        total = jnp.zeros((R, E), jnp.float32)
        match = jnp.zeros((R, E), jnp.float32)
        for z in range(N_ZH):
            k = keys_ref[z * R : (z + 1) * R]
            e = jnp.exp2(scores(q, k) * SCALE)
            e = jnp.where(itself == (x - piece) * GATHERED + (z - zh) * R, 0.0, e)
            exp_ref[rows, z * R : (z + 1) * R] = e.astype(jnp.bfloat16)
            chosen = jnp.where(partner == z * R, 1.0, 0.0).astype(jnp.bfloat16)
            match = match + jnp.dot(chosen, k, preferred_element_type=jnp.float32)
            total = total + fold(e)
        match_ref[rows] = match.astype(jnp.bfloat16)
        lines.append(as_lines(lane_sums(total)))
        match = match * q.astype(jnp.float32)
        positive = positive + jnp.sum(match.reshape(R // 8, 8, E), axis=0)
    positive = jnp.broadcast_to(jnp.sum(positive, axis=(0, 1), keepdims=True), (16 - SLOT, E))
    sums_ref[...] = jnp.concatenate(lines + [positive], axis=0)


def others_kernel(queries_ref, keys_ref, own_ref, exp_ref, line_ref, total):
    for t in range(ROUNDS):
        for z in range(N_ZH):
            k = far_keys(keys_ref, t, z)
            at = (t * N_ZH + z) * R
            for piece in range(N_X):
                rows = slice(piece * R, (piece + 1) * R)
                e = jnp.exp2(scores(queries_ref[piece, 0:R], k) * SCALE)
                exp_ref[rows, at : at + R] = e.astype(jnp.bfloat16)
                total[rows] = fold(e) + total[rows] if at > 0 else fold(e)
    sums = lane_sums(total[...])
    lines = [sums[0:1, i * E : (i + 1) * E] for i in range(N_X * LINES)]
    lines = jnp.concatenate(lines + [jnp.zeros((16 - SLOT, E), jnp.float32)], axis=0) + own_ref[...]
    for i in range(N_BLOCK):
        line_ref[i] = lines


def sums_kernel(line_ref, level_ref, mine_ref, log_ref, held):
    near = lax.axis_index("y") * 2 + lax.axis_index("c")
    x = lax.axis_index("x")
    slot = lax.broadcasted_iota(jnp.int32, (16, E), 0)
    loss = jnp.zeros((16, E), jnp.float32)
    for i in range(NEAR):
        y, c = divmod(i, 2)
        at = (c * 4 + y) * N_X
        part = line_ref[at]
        for j in range(1, N_X):
            part = part + line_ref[at + j]
        sums = jnp.where(slot < SLOT, part, 1.0)
        logs = jnp.log(sums)
        loss = loss + jnp.where(slot < SLOT, logs, 0.0)
        loss = loss - jnp.where(slot == SLOT, part * (INVERSE_TAU / E), 0.0)
        held[i, 0] = 1.0 / sums
        held[i, 1] = logs
    mine_ref[...] = held[near, 0]
    log_ref[...] = held[near, 1, pl.ds(x * LINES, LINES), :]
    level = [held[i, 0, pl.ds(x * LINES, LINES), :] for i in range(NEAR)]
    loss = jnp.broadcast_to(jnp.sum(loss, axis=(0, 1), keepdims=True), (1, E))
    for _ in range(3):
        level.append(loss.astype(jnp.bfloat16).astype(jnp.float32))
        loss = loss - level[-1]
    level.append(jnp.zeros((32 - LOSS - 3, E), jnp.float32))
    level = jnp.concatenate(level, axis=0).astype(jnp.bfloat16)
    for i in range(N_ZH * N_ZL):
        level_ref[i] = level


def direction_kernel(
    plan_ref, own_ref, others_ref, keys_ref, far_ref, match_ref, mine_ref, sums_ref, out_ref, loss_ref, held, both
):
    zu, zl, y, c = (lax.axis_index(a) for a in BLOCK)
    here = ((zu * 2 + zl) * 4 + y) * 2 + c
    held[...] = sums_ref[...].astype(jnp.float32)
    loss = held[0, LOSS : LOSS + 3, :]
    for i in range(1, N_ZH * N_ZL):
        loss = loss + held[i, LOSS : LOSS + 3, :]
    loss_ref[...] = jnp.sum(loss, axis=0, keepdims=True)[:, 0:1] / (N_BLOCK * BLOCK_ROWS)
    for t in range(ROUNDS + 1):
        other = here if t == 0 else plan_ref[t - 1, here]
        level = other // NEAR
        near = other - level * NEAR
        for z in range(N_ZH):
            inverse = to_column(as_row(held[level * N_ZH + z, pl.ds(near * LINES, LINES), :]))
            k = keys_ref[z * R : (z + 1) * R] if t == 0 else far_keys(far_ref, t - 1, z)
            at = (t * N_ZH + z) * R
            both[at : at + R, 0:E] = k
            both[at : at + R, E : 2 * E] = (k.astype(jnp.float32) * inverse).astype(jnp.bfloat16)
    for piece in range(N_X):
        rows = slice(piece * R, (piece + 1) * R)
        total = jnp.dot(own_ref[rows], both[0:GATHERED], preferred_element_type=jnp.float32)
        total = total + jnp.dot(others_ref[rows], both[GATHERED:], preferred_element_type=jnp.float32)
        column = to_column(as_row(mine_ref[piece * LINES : (piece + 1) * LINES, :]))
        out_ref[piece] = column * total[:, 0:E] + total[:, E : 2 * E] - 2.0 * match_ref[rows].astype(jnp.float32)


def finish_kernel(embed_ref, parts_ref, out_ref):
    x = embed_ref[...]
    inverse = lax.rsqrt(jnp.sum(x * x, axis=1, keepdims=True) + 1e-06)
    unit = x * inverse
    total = parts_ref[0]
    for i in range(1, N_X):
        total = total + parts_ref[i]
    direction = INVERSE_TAU * total
    out_ref[...] = inverse * (direction - unit * jnp.sum(unit * direction, axis=1, keepdims=True))


def f32(*shape):
    return jax.ShapeDtypeStruct(shape, jnp.float32)


def bf16(*shape):
    return jax.ShapeDtypeStruct(shape, jnp.bfloat16)


def exchange(value, axes):
    return lax.all_to_all(value, axes, 0, 0, tiled=True)


def call(kernel, out_shape, *args, specs=None, **more):
    return pl.pallas_call(
        kernel,
        out_shape=out_shape,
        in_specs=specs or [whole] * len(args),
        out_specs=(whole,) * len(out_shape) if isinstance(out_shape, tuple) else whole,
        compiler_params=pltpu.CompilerParams(vmem_limit_bytes=VMEM),
        **more,
    )(*args)


def cost(keys):
    pairs = N_X * R * keys
    return pl.CostEstimate(flops=2 * pairs * E, bytes_accessed=2 * pairs, transcendentals=pairs)


def body(embed, partner, plan):
    far = ROUNDS * GATHERED
    with jax.named_scope("normalize"):
        given = (embed, partner.reshape(LINES, E), plan)
        rounded, sent, plan = pl.pallas_call(
            normalize_kernel,
            grid=(1,),
            out_shape=(bf16(R, E), bf16(SENT, E), jax.ShapeDtypeStruct(plan.shape, plan.dtype)),
            in_specs=[pl.BlockSpec(array.shape, lambda g: (0, 0)) for array in given],
            out_specs=(whole, whole, whole),
        )(*given)
    with jax.named_scope("own"):
        keys = lax.all_gather(rounded, "zh", axis=0, tiled=True)
    with jax.named_scope("queries"):
        queries = lax.all_gather(sent, "x", axis=0)
    with jax.named_scope("opponents"):
        chunks = keys.reshape(N_HALF, CHUNK, E)
        chunks = exchange(jnp.concatenate([chunks, chunks]), BLOCK)
        chosen = call(select_kernel, bf16(N_HALF, ROUNDS, CHUNK, E), plan, chunks, queries, specs=[smem, whole, anywhere])
        others = exchange(chosen, HALF)
    with jax.named_scope("own"):
        own_exps, match, own_sums = call(
            own_kernel,
            (bf16(N_X * R, GATHERED), bf16(N_X * R, E), f32(16, E)),
            queries,
            keys,
            cost_estimate=cost(GATHERED),
        )
    with jax.named_scope("others"):
        exps, line = call(
            others_kernel,
            (bf16(N_X * R, far), f32(N_BLOCK, 16, E)),
            queries,
            others,
            own_sums,
            scratch_shapes=[pltpu.VMEM((N_X * R, E), jnp.float32)],
            cost_estimate=cost(far),
        )
    with jax.named_scope("sums"):
        line = exchange(line, PLANE)
        level, mine, log_partition = call(
            sums_kernel,
            (bf16(N_ZH * N_ZL, 32, E), f32(16, E), f32(LINES, E)),
            line,
            scratch_shapes=[pltpu.VMEM((NEAR, 2, 16, E), jnp.float32)],
        )
        level = exchange(level, COLUMN)
    with jax.named_scope("direction"):
        parts, loss = call(
            direction_kernel,
            (f32(N_X, R, E), f32(1, 1)),
            plan,
            own_exps,
            exps,
            keys,
            others,
            match,
            mine,
            level,
            specs=[smem] + [whole] * 7,
            scratch_shapes=[
                pltpu.VMEM((N_ZH * N_ZL, 32, E), jnp.float32),
                pltpu.VMEM((GATHERED + far, 2 * E), jnp.bfloat16),
            ],
            cost_estimate=cost(GATHERED + far),
        )
        parts = exchange(parts, "x")
    with jax.named_scope("finish"):
        grad = call(finish_kernel, f32(R, E), embed, parts)
    return (grad, log_partition.reshape(R), loss.reshape(()))


def solution(mesh):
    split = Mesh(mesh.devices.reshape(SIZES), AXES)
    return jax.shard_map(
        body,
        mesh=split,
        in_specs=(P(AXES, None), P(AXES), P()),
        out_specs=(P(AXES, None), P(AXES), P()),
        check_vma=False,
    )
```

```python
import jax
import jax.numpy as jnp
import numpy as np
from jax import lax
from jax.experimental import pallas as pl
from jax.experimental.pallas import tpu as pltpu
from jax.sharding import Mesh
from jax.sharding import PartitionSpec as P

ROUNDS = 2
INVERSE_TAU = 10.0
SCALE = INVERSE_TAU * float(np.log2(np.e))

AXES = ("zu", "zl", "y", "c", "x", "zh")
SIZES = (2, 2, 4, 2, 4, 4)
BLOCK = ("zu", "zl", "y", "c")
HALF = ("zl", "y", "c")
PLANE = ("c", "y", "x")
COLUMN = ("zu", "zl", "zh")

R = 384
E = 128
N_BLOCK = 32
N_X = 4
N_ZL = 4
N_ZH = 4
GATHERED = R * N_ZH
BLOCK_ROWS = GATHERED * N_X
N_HALF = N_BLOCK // 2
CHUNK = GATHERED // N_HALF
SENT = R + 16
LINES = R // E
SLOT = LINES * N_X
NEAR = 8
LOSS = LINES * NEAR
VMEM = 5 * 1024 * 1024

whole = pl.BlockSpec(memory_space=pltpu.VMEM)
smem = pl.BlockSpec(memory_space=pltpu.SMEM)


def as_row(lines):
    return jnp.concatenate([lines[i : i + 1] for i in range(LINES)], axis=1)


def as_lines(row):
    return jnp.concatenate([row[0:1, i * E : (i + 1) * E] for i in range(LINES)], axis=0)


def to_column(row):
    return jnp.transpose(jnp.broadcast_to(row, (E, R)))


def widen(wide):
    return jnp.concatenate([wide] * LINES, axis=1)


def lane_sums(value):
    return jnp.sum(jnp.transpose(value), axis=0, keepdims=True)


def scores(q, k):
    return lax.dot_general(q, k, (((1,), (1,)), ((), ())), preferred_element_type=jnp.float32)


def fold(e):
    part = e[:, 0:E]
    for i in range(1, LINES):
        part = part + e[:, i * E : (i + 1) * E]
    return part


def far_keys(keys_ref, t, z):
    each = R // CHUNK
    return jnp.concatenate([keys_ref[z * each + i, t] for i in range(each)], axis=0)


def normalize_kernel(embed_ref, partner_ref, plan_ref, rounded_ref, sent_ref, copy_ref):
    x = embed_ref[...]
    inverse = lax.rsqrt(jnp.sum(x * x, axis=1, keepdims=True) + 1e-06)
    rounded = (x * inverse).astype(jnp.bfloat16)
    rounded_ref[...] = rounded
    index = partner_ref[...]
    high = index // 128
    low = index - high * 128
    both = jnp.concatenate([high, low, jnp.zeros((16 - 2 * LINES, E), jnp.int32)], axis=0)
    index = both.astype(jnp.float32).astype(jnp.bfloat16)
    sent_ref[0:R] = rounded
    sent_ref[R:SENT] = index
    copy_ref[...] = plan_ref[...]


def select_kernel(plan_ref, chunks_ref, out_ref):
    first = lax.axis_index("zu") * N_HALF
    for start in range(0, N_HALF, 4):
        several = range(start, start + 4)
        taken = [[chunks_ref[plan_ref[t, first + b]] for t in range(ROUNDS)] for b in several]
        for b in several:
            for t in range(ROUNDS):
                out_ref[b, t] = taken[b - start][t]


def own_kernel(queries_ref, keys_ref, plan_ref, exp_ref, match_ref, sums_ref, copy_ref):
    copy_ref[...] = plan_ref[...]
    x = lax.axis_index("x")
    zh = lax.axis_index("zh")
    lane = lax.broadcasted_iota(jnp.int32, (R, R), 1)
    itself = lax.broadcasted_iota(jnp.int32, (R, R), 0) - lane
    positive = jnp.zeros((8, E), jnp.float32)
    lines = []
    for piece in range(N_X):
        q = queries_ref[piece, 0:R]
        rows = slice(piece * R, (piece + 1) * R)
        index = queries_ref[piece, R:SENT].astype(jnp.float32)
        index = as_row(index[0:LINES]) * 128.0 + as_row(index[LINES : 2 * LINES])
        partner = widen(to_column(index)).astype(jnp.int32) - x * GATHERED - lane
        total = jnp.zeros((R, E), jnp.float32)
        match = jnp.zeros((R, E), jnp.float32)
        for z in range(N_ZH):
            k = keys_ref[z * R : (z + 1) * R]
            e = jnp.exp2(scores(q, k) * SCALE)
            e = jnp.where(itself == (x - piece) * GATHERED + (z - zh) * R, 0.0, e)
            exp_ref[rows, z * R : (z + 1) * R] = e.astype(jnp.bfloat16)
            chosen = jnp.where(partner == z * R, 1.0, 0.0).astype(jnp.bfloat16)
            match = match + jnp.dot(chosen, k, preferred_element_type=jnp.float32)
            total = total + fold(e)
        match_ref[rows] = match.astype(jnp.bfloat16)
        lines.append(as_lines(lane_sums(total)))
        match = match * q.astype(jnp.float32)
        positive = positive + jnp.sum(match.reshape(R // 8, 8, E), axis=0)
    positive = jnp.broadcast_to(jnp.sum(positive, axis=(0, 1), keepdims=True), (16 - SLOT, E))
    sums_ref[...] = jnp.concatenate(lines + [positive], axis=0)


def others_kernel(queries_ref, keys_ref, own_ref, exp_ref, line_ref, total):
    for t in range(ROUNDS):
        for z in range(N_ZH):
            k = far_keys(keys_ref, t, z)
            at = (t * N_ZH + z) * R
            for piece in range(N_X):
                rows = slice(piece * R, (piece + 1) * R)
                e = jnp.exp2(scores(queries_ref[piece, 0:R], k) * SCALE)
                exp_ref[rows, at : at + R] = e.astype(jnp.bfloat16)
                total[rows] = fold(e) + total[rows] if at > 0 else fold(e)
    sums = lane_sums(total[...])
    lines = [sums[0:1, i * E : (i + 1) * E] for i in range(N_X * LINES)]
    lines = jnp.concatenate(lines + [jnp.zeros((16 - SLOT, E), jnp.float32)], axis=0) + own_ref[...]
    for i in range(N_BLOCK):
        line_ref[i] = lines


def sums_kernel(line_ref, level_ref, mine_ref, log_ref, held):
    near = lax.axis_index("y") * 2 + lax.axis_index("c")
    x = lax.axis_index("x")
    slot = lax.broadcasted_iota(jnp.int32, (16, E), 0)
    loss = jnp.zeros((16, E), jnp.float32)
    for i in range(NEAR):
        y, c = divmod(i, 2)
        at = (c * 4 + y) * N_X
        part = line_ref[at]
        for j in range(1, N_X):
            part = part + line_ref[at + j]
        sums = jnp.where(slot < SLOT, part, 1.0)
        logs = jnp.log(sums)
        loss = loss + jnp.where(slot < SLOT, logs, 0.0)
        loss = loss - jnp.where(slot == SLOT, part * (INVERSE_TAU / E), 0.0)
        held[i, 0] = 1.0 / sums
        held[i, 1] = logs
    mine_ref[...] = held[near, 0]
    log_ref[...] = held[near, 1, pl.ds(x * LINES, LINES), :]
    level = [held[i, 0, pl.ds(x * LINES, LINES), :] for i in range(NEAR)]
    loss = jnp.broadcast_to(jnp.sum(loss, axis=(0, 1), keepdims=True), (1, E))
    for _ in range(3):
        level.append(loss.astype(jnp.bfloat16).astype(jnp.float32))
        loss = loss - level[-1]
    level.append(jnp.zeros((32 - LOSS - 3, E), jnp.float32))
    level = jnp.concatenate(level, axis=0).astype(jnp.bfloat16)
    for i in range(N_ZH * N_ZL):
        level_ref[i] = level


def direction_kernel(
    plan_ref, own_ref, others_ref, keys_ref, far_ref, match_ref, mine_ref, sums_ref, out_ref, loss_ref, held, both
):
    zu, zl, y, c = (lax.axis_index(a) for a in BLOCK)
    here = ((zu * 2 + zl) * 4 + y) * 2 + c
    held[...] = sums_ref[...].astype(jnp.float32)
    loss = held[0, LOSS : LOSS + 3, :]
    for i in range(1, N_ZH * N_ZL):
        loss = loss + held[i, LOSS : LOSS + 3, :]
    loss_ref[...] = jnp.sum(loss, axis=0, keepdims=True)[:, 0:1] / (N_BLOCK * BLOCK_ROWS)
    for t in range(ROUNDS + 1):
        other = here if t == 0 else plan_ref[t - 1, here]
        level = other // NEAR
        near = other - level * NEAR
        for z in range(N_ZH):
            inverse = to_column(as_row(held[level * N_ZH + z, pl.ds(near * LINES, LINES), :]))
            k = keys_ref[z * R : (z + 1) * R] if t == 0 else far_keys(far_ref, t - 1, z)
            at = (t * N_ZH + z) * R
            both[at : at + R, 0:E] = k
            both[at : at + R, E : 2 * E] = (k.astype(jnp.float32) * inverse).astype(jnp.bfloat16)
    for piece in range(N_X):
        rows = slice(piece * R, (piece + 1) * R)
        total = jnp.dot(own_ref[rows], both[0:GATHERED], preferred_element_type=jnp.float32)
        total = total + jnp.dot(others_ref[rows], both[GATHERED:], preferred_element_type=jnp.float32)
        column = to_column(as_row(mine_ref[piece * LINES : (piece + 1) * LINES, :]))
        out_ref[piece] = column * total[:, 0:E] + total[:, E : 2 * E] - 2.0 * match_ref[rows].astype(jnp.float32)


def finish_kernel(embed_ref, parts_ref, out_ref):
    x = embed_ref[...]
    inverse = lax.rsqrt(jnp.sum(x * x, axis=1, keepdims=True) + 1e-06)
    unit = x * inverse
    total = parts_ref[0]
    for i in range(1, N_X):
        total = total + parts_ref[i]
    direction = INVERSE_TAU * total
    out_ref[...] = inverse * (direction - unit * jnp.sum(unit * direction, axis=1, keepdims=True))


def f32(*shape):
    return jax.ShapeDtypeStruct(shape, jnp.float32)


def bf16(*shape):
    return jax.ShapeDtypeStruct(shape, jnp.bfloat16)


def exchange(value, axes):
    return lax.all_to_all(value, axes, 0, 0, tiled=True)


def call(kernel, out_shape, *args, specs=None, **more):
    return pl.pallas_call(
        kernel,
        out_shape=out_shape,
        in_specs=specs or [whole] * len(args),
        out_specs=(whole,) * len(out_shape) if isinstance(out_shape, tuple) else whole,
        compiler_params=pltpu.CompilerParams(vmem_limit_bytes=VMEM),
        **more,
    )(*args)


def cost(keys):
    pairs = N_X * R * keys
    return pl.CostEstimate(flops=2 * pairs * E, bytes_accessed=2 * pairs, transcendentals=pairs)


def body(embed, partner, plan):
    far = ROUNDS * GATHERED
    with jax.named_scope("normalize"):
        given = (embed, partner.reshape(LINES, E), plan)
        rounded, sent, plan = pl.pallas_call(
            normalize_kernel,
            grid=(1,),
            out_shape=(bf16(R, E), bf16(SENT, E), jax.ShapeDtypeStruct(plan.shape, plan.dtype)),
            in_specs=[pl.BlockSpec(array.shape, lambda g: (0, 0)) for array in given],
            out_specs=(whole, whole, whole),
        )(*given)
    with jax.named_scope("own"):
        keys = lax.all_gather(rounded, "zh", axis=0, tiled=True)
    with jax.named_scope("queries"):
        queries = lax.all_gather(sent, "x", axis=0)
    with jax.named_scope("own"):
        own_exps, match, own_sums, plan = call(
            own_kernel,
            (bf16(N_X * R, GATHERED), bf16(N_X * R, E), f32(16, E), jax.ShapeDtypeStruct(plan.shape, plan.dtype)),
            queries,
            keys,
            plan,
            cost_estimate=cost(GATHERED),
        )
    with jax.named_scope("opponents"):
        chunks = jnp.broadcast_to(keys.reshape(N_HALF, CHUNK, E), (2, N_HALF, CHUNK, E))
        chunks = exchange(chunks.reshape(N_BLOCK, CHUNK, E), BLOCK)
        chosen = call(select_kernel, bf16(N_HALF, ROUNDS, CHUNK, E), plan, chunks, specs=[smem, whole])
        others = exchange(chosen, HALF)
    with jax.named_scope("others"):
        exps, line = call(
            others_kernel,
            (bf16(N_X * R, far), f32(N_BLOCK, 16, E)),
            queries,
            others,
            own_sums,
            scratch_shapes=[pltpu.VMEM((N_X * R, E), jnp.float32)],
            cost_estimate=cost(far),
        )
    with jax.named_scope("sums"):
        line = exchange(line, PLANE)
        level, mine, log_partition = call(
            sums_kernel,
            (bf16(N_ZH * N_ZL, 32, E), f32(16, E), f32(LINES, E)),
            line,
            scratch_shapes=[pltpu.VMEM((NEAR, 2, 16, E), jnp.float32)],
        )
        level = exchange(level, COLUMN)
    with jax.named_scope("direction"):
        parts, loss = call(
            direction_kernel,
            (f32(N_X, R, E), f32(1, 1)),
            plan,
            own_exps,
            exps,
            keys,
            others,
            match,
            mine,
            level,
            specs=[smem] + [whole] * 7,
            scratch_shapes=[
                pltpu.VMEM((N_ZH * N_ZL, 32, E), jnp.float32),
                pltpu.VMEM((GATHERED + far, 2 * E), jnp.bfloat16),
            ],
            cost_estimate=cost(GATHERED + far),
        )
        parts = exchange(parts, "x")
    with jax.named_scope("finish"):
        grad = call(finish_kernel, f32(R, E), embed, parts)
    return (grad, log_partition.reshape(R), loss.reshape(()))


def solution(mesh):
    split = Mesh(mesh.devices.reshape(SIZES), AXES)
    return jax.shard_map(
        body,
        mesh=split,
        in_specs=(P(AXES, None), P(AXES), P()),
        out_specs=(P(AXES, None), P(AXES), P()),
        check_vma=False,
    )
```
